512 devices in a mesh: space: 64 (over x, z_hi, y, core), vel: 8 (over z_lo).
Axes of the slice: x: 4, y: 4, z: 16 (z_hi: 2, z_lo: 8; z = z_hi * 8 + z_lo), core: 2. Of those that a mesh axis runs over, the one named last changes fastest.
Arguments:
- density: float32 [128, 16, 4, 4096], P('space', None, None, 'vel'), may hold values from 0.2 to 2
- gain_left: float32 [4, 4096], replicated, may hold values from -4 to 4
- gain_right: float32 [4, 4096], replicated, may hold values from -4 to 4
- loss_kernel: float32 [4096], replicated, may hold values from -4 to 4
Outputs:
- evolved: float32 [128, 16, 4, 4096], P('space', None, None, 'vel')
The draws below stay inside these ranges and needn't reach their ends.
All inputs are finite; a program needn't handle non-finite values.
Results may differ from the reference program's by a relative error of at most 0.0003.
Values sent between devices are 32-bit elements; how exact they have to be, the bound alone decides.
A program may use at most 64 MiB of HBM per device.

```python
import math
import jax
import jax.numpy as jnp
from jax import lax

M = 16
TERMS = 4
NY = 16
NZ = 4
NX = 128
SPEEDS = 4096


def block_levels(stream_key, extent, pieces, smallest, high):
    level = 1.0
    for axis_at, blocks in pieces:
        heights = jax.random.uniform(jax.random.fold_in(jax.random.fold_in(stream_key, 6), axis_at), (blocks,), jnp.float32, smallest / len(pieces), high / len(pieces))
        level = level * jnp.repeat(jnp.exp(heights), extent[axis_at] // blocks).reshape((-1,) + (1,) * (len(extent) - 1 - axis_at))
    return level


def scatter_about(rng, dims, scale, bound, held_as=jnp.bfloat16):
    result = jax.random.normal(rng, dims, jnp.float32) * scale
    return jnp.minimum(jnp.maximum(result, -bound), bound).astype(held_as)


def setup_inputs(seed: int = 0) -> dict:
    arg_keys = jax.random.split(jax.random.key(seed), 5)
    return {
        "density": jnp.clip(jnp.exp(math.log(2.0) - 2.3025851 * jax.random.uniform(arg_keys[0], (NX, NY, NZ, SPEEDS), jnp.float32) ** block_levels(arg_keys[0], (NX, NY, NZ, SPEEDS), ((0, 64), (3, 8)), -0.2, 0.2)), 0.2, 2.0),
        "gain_left": scatter_about(arg_keys[1], (TERMS, SPEEDS), 0.6, 4.0, jnp.float32),
        "gain_right": scatter_about(arg_keys[2], (TERMS, SPEEDS), 0.6, 4.0, jnp.float32),
        "loss_kernel": scatter_about(arg_keys[3], (SPEEDS,), 0.6, 4.0, jnp.float32),
    }


courant = 1.0 / 6.0
time_step = 0.25
rate_scale = 0.25

def minmod(lower_diff, upper_diff):
    smaller = jnp.minimum(jnp.abs(lower_diff), jnp.abs(upper_diff))
    return jnp.where(lower_diff * upper_diff > 0.0, jnp.sign(lower_diff) * smaller, 0.0)

def face_jump(back_two, back_one, middle, ahead_one, ahead_two, positive):
    d_back = middle - back_one
    d_ahead = ahead_one - middle
    d_far_back = back_one - back_two
    d_far_ahead = ahead_two - ahead_one
    right_up = middle + 0.5 * minmod(d_back, d_ahead)
    left_up = back_one + 0.5 * minmod(d_far_back, d_back)
    right_down = ahead_one - 0.5 * minmod(d_ahead, d_far_ahead)
    left_down = middle - 0.5 * minmod(d_back, d_ahead)
    return jnp.where(positive, right_up - left_up, right_down - left_down)

def rolled_jump(field_now, roll_axis, positive):
    return face_jump(jnp.roll(field_now, 2, roll_axis), jnp.roll(field_now, 1, roll_axis), field_now, jnp.roll(field_now, -1, roll_axis), jnp.roll(field_now, -2, roll_axis), positive)

def velocity(counter, grid_side):
    return (2.0 * counter.astype(jnp.float32) + 1.0) / grid_side - 1.0

def transport_all(field_now):
    pair_index = jnp.arange(M * M, dtype=jnp.int32)
    vel_x = velocity(pair_index // M, M)
    vel_y = velocity(pair_index % M, M)
    vel_z = velocity(jnp.arange(M, dtype=jnp.int32), M)
    stacked = jnp.moveaxis(field_now.reshape(NX, NY, NZ, M, M * M), 3, 0)

    def advect_plane(inputs_pair):
        slab_block, speed_z = inputs_pair
        jump_x = rolled_jump(slab_block, 0, vel_x > 0.0)
        jump_y = rolled_jump(slab_block, 1, vel_y > 0.0)
        jump_z = rolled_jump(slab_block, 2, speed_z > 0.0)
        return slab_block - courant * (vel_x * jump_x + vel_y * jump_y + speed_z * jump_z)
    moved = lax.map(advect_plane, (stacked, vel_z))
    return jnp.moveaxis(moved, 0, 3).reshape(field_now.shape)

def collide(cell_rows, gain_left, gain_right, loss_kernel):
    spectra_in = cell_rows.reshape(-1, M, M, M)
    spectrum = jnp.fft.fftn(spectra_in, axes=(1, 2, 3))
    gain = jnp.zeros(spectra_in.shape, jnp.float32)
    for term_index in range(TERMS):
        left_term = jnp.fft.ifftn(gain_left[term_index].reshape(M, M, M) * spectrum, axes=(1, 2, 3))
        right_term = jnp.fft.ifftn(gain_right[term_index].reshape(M, M, M) * spectrum, axes=(1, 2, 3))
        gain = gain + (left_term.real * right_term.real - left_term.imag * right_term.imag)
    loss = spectra_in * jnp.fft.ifftn(loss_kernel.reshape(M, M, M) * spectrum, axes=(1, 2, 3)).real
    return (gain - loss).reshape(cell_rows.shape)

def reference(density, gain_left, gain_right, loss_kernel):
    speed_index = jnp.arange(M ** 3, dtype=jnp.int32)
    speed_z = velocity(speed_index // (M * M), M)
    speed_x = velocity(speed_index // M % M, M)
    speed_y = velocity(speed_index % M, M)
    speed_sq = speed_x * speed_x + speed_y * speed_y + speed_z * speed_z
    advected = transport_all(density)
    change = lax.map(lambda plane_rows: collide(plane_rows, gain_left, gain_right, loss_kernel), advected.reshape(NX, NY * NZ, M ** 3)).reshape(advected.shape)
    weight = (2.0 / M) ** 3
    mass_total = lax.optimization_barrier(jnp.sum(advected, -1)) * weight
    mean_flow_first = lax.optimization_barrier(jnp.sum(advected * speed_x, -1)) * weight / mass_total
    mean_flow_second = lax.optimization_barrier(jnp.sum(advected * speed_y, -1)) * weight / mass_total
    mean_flow_third = lax.optimization_barrier(jnp.sum(advected * speed_z, -1)) * weight / mass_total
    kinetic_content = lax.optimization_barrier(jnp.sum(advected * speed_sq, -1)) * weight / mass_total
    cell_heat_level = (kinetic_content - (mean_flow_first * mean_flow_first + mean_flow_second * mean_flow_second + mean_flow_third * mean_flow_third)) / 3.0
    gaussian_variance = 2.0 * math.pi * cell_heat_level
    gaussian_prefactor = mass_total / (gaussian_variance * jnp.sqrt(gaussian_variance))
    relative_motion_squared = (speed_x - mean_flow_first[..., None]) ** 2 + (speed_y - mean_flow_second[..., None]) ** 2 + (speed_z - mean_flow_third[..., None]) ** 2
    equilibrium_profile = gaussian_prefactor[..., None] * jnp.exp(-relative_motion_squared / (2.0 * cell_heat_level[..., None]))
    rate = (rate_scale * mass_total)[..., None]
    relaxed = (advected + time_step * change + time_step * rate * equilibrium_profile) / (1.0 + time_step * rate)
    return transport_all(relaxed)
```

```python
import math

import jax
import jax.numpy as jnp
import numpy as np
from jax import lax
from jax.experimental import pallas as pl
from jax.experimental.pallas import tpu as pltpu
from jax.sharding import PartitionSpec as P

MESH = pl.DeviceIdType.MESH
M = 16
NP = 8
CH = 2
courant = 1.0 / 6.0
time_step = 0.25
rate_scale = 0.25
f32 = jnp.float32
bf16 = jnp.bfloat16


def times_root(re, im, k, n, sign):
    k = k % n
    if k == 0:
        return re, im
    if 4 * k == n:
        return (-im, re) if sign > 0 else (im, -re)
    if 2 * k == n:
        return -re, -im
    if 4 * k == 3 * n:
        return (im, -re) if sign > 0 else (-im, re)
    c, s = math.cos(2 * math.pi * k / n), sign * math.sin(2 * math.pi * k / n)
    if 8 * k % n == 0:
        r = math.sqrt(0.5)
        cs, ss = (1 if c > 0 else -1), (1 if s > 0 else -1)
        a = re if cs > 0 else -re
        b = im if ss > 0 else -im
        d = re if ss > 0 else -re
        e = im if cs > 0 else -im
        return (a - b) * r, (d + e) * r
    return re * c - im * s, re * s + im * c


def transform(values, sign):
    n = len(values)
    if n == 1:
        return values
    even = transform(values[0::2], sign)
    odd = transform(values[1::2], sign)
    out = [None] * n
    for k in range(n // 2):
        tr, ti = times_root(*odd[k], k, n, sign)
        er, ei = even[k]
        out[k] = (er + tr, ei + ti)
        out[k + n // 2] = (er - tr, ei - ti)
    return out


def real_transform(values):
    n = len(values)
    if n == 1:
        return [(values[0], None)]
    if n == 2:
        return [(values[0] + values[1], None), (values[0] - values[1], None)]
    even = real_transform(values[0::2])
    odd = real_transform(values[1::2])
    out = [None] * (n // 2 + 1)
    h = n // 2
    for k in range(n // 4 + 1):
        er, ei = even[k]
        o_r, o_i = odd[k]
        if k == 0:
            out[0] = (er + o_r, None)
            out[h] = (er - o_r, None)
        elif k == n // 4:
            out[k] = (er, -o_r)
        else:
            tr, ti = times_root(o_r, o_i, k, n, -1)
            out[k] = (er + tr, ei + ti)
            out[h - k] = (er - tr, ti - ei)
    return out


def minmod(p, q):
    return jnp.minimum(jnp.maximum(p, jnp.minimum(q, 0.0)), jnp.maximum(q, 0.0))


def turned(v, by):
    n = v.shape[-2]
    if by > 0:
        return jnp.concatenate([v[..., n - 1 :, :], v[..., : n - 1, :]], axis=-2)
    return jnp.concatenate([v[..., 1:, :], v[..., :1, :]], axis=-2)


def moved(g, low, high, positive, vel_x, vel_y, vel_z, zs):
    sign = 0.5 if positive else -0.5
    here = g[zs[0] : zs[-1] + 1]
    planes = jnp.concatenate([low, here, high], axis=1)
    d = planes[:, 1:] - planes[:, :-1]
    face = planes[:, 1:4] + sign * minmod(d[:, :-1], d[:, 1:])
    jump_x = face[:, 1:] - face[:, :-1]

    up_y = vel_y > 0.0
    half_y = jnp.where(up_y, 0.5, -0.5)
    d = here - turned(here, 1)
    face = here + half_y * minmod(d, turned(d, -1))
    e = face - turned(face, 1)
    jump_y = jnp.where(up_y, e, turned(e, -1))

    up_z = vel_z > 0.0
    half_z = jnp.where(up_z, 0.5, -0.5)
    d = [g[z] - g[(z + 3) % 4] for z in range(4)]
    face = [g[z] + half_z * minmod(d[z], d[(z + 1) % 4]) for z in range(4)]
    e = [face[z] - face[(z + 3) % 4] for z in range(4)]
    jump_z = jnp.stack([jnp.where(up_z, e[z], e[(z + 1) % 4]) for z in zs])
    return here - courant * (vel_x * jump_x + vel_y * jump_y + vel_z * jump_z)


def lane_velocities(c_hi):
    lane = lax.broadcasted_iota(jnp.int32, (1, 128), 1)
    vel_x = (2.0 * ((lane >> 4) + 8 * c_hi).astype(f32) + 1.0) / M - 1.0
    vel_y = (2.0 * (lane & 15).astype(f32) + 1.0) / M - 1.0
    return vel_x, vel_y


def level(a):
    return (2.0 * a.astype(f32) + 1.0) / M - 1.0


def split(v):
    hi = v.astype(bf16)
    lo = (v - hi.astype(f32)).astype(bf16)
    return hi, lo


def product(v, weights):
    hi, lo = split(v)
    return jnp.dot(
        jnp.concatenate([hi, lo, hi], axis=1), weights, preferred_element_type=f32
    )


def wide(v):
    return jnp.concatenate([v[0], v[1]], axis=1)


def relaxed_cells(k, x_ref, tables, w_forward, w_inverse, spec, gain, out_ref):
    rows = [wide(x_ref[k, a]) * (1.0 / M**3) for a in range(M)]
    modes = real_transform(rows)
    parts = [re for re, _ in modes] + [im for _, im in modes[1:8]]
    both = product(jnp.concatenate(parts, axis=0), w_forward[...])
    both = [both[8 * i : 8 * i + 8] for i in range(16)]
    for q in range(9):
        rc, rs = both[q][:, :256], both[q][:, 256:]
        if q in (0, 8):
            spec[q, 0] = rc
            spec[q, 1] = -rs
            continue
        ic, js = both[q + 8][:, :256], both[q + 8][:, 256:]
        spec[q, 0] = rc + js
        spec[q, 1] = ic - rs
        spec[16 - q, 0] = rc - js
        spec[16 - q, 1] = -ic - rs

    def bent(m):
        values = []
        for q in range(M):
            t = tables[m, q]
            values.append((t * spec[q, 0], t * spec[q, 1]))
        values = transform(values, 1)
        return jnp.concatenate(
            [jnp.concatenate([re, im], axis=1) for re, im in values], axis=0
        )

    loss = product(bent(8), w_inverse[:, :256])
    gain[...] = -(jnp.concatenate([wide(x_ref[k, a]) for a in range(M)], axis=0) * loss)

    def term(p, c):
        both = product(jnp.concatenate([bent(p), bent(p + 4)], axis=0), w_inverse[...])
        left, right = both[:128], both[128:]
        gain[...] += left[:, :256] * right[:, :256] - left[:, 256:] * right[:, 256:]
        return c

    lax.fori_loop(0, 4, term, 0)

    velocities = [lane_velocities(c) for c in range(2)]
    weight = (2.0 / M) ** 3
    vz = [(2.0 * a + 1.0) / M - 1.0 for a in range(M)]
    cells = [x_ref[k, a] for a in range(M)]
    s0 = sum(cells[1:], cells[0])
    s1 = sum((cells[a] * vz[a] for a in range(1, M)), cells[0] * vz[0])
    s2 = sum((cells[a] * (vz[a] * vz[a]) for a in range(1, M)), cells[0] * (vz[0] * vz[0]))

    def total(v):
        return jnp.sum(v, axis=-1, keepdims=True) * weight

    (vx0, vy0), (vx1, vy1) = velocities
    mass = total(s0[0] + s0[1])
    mean_x = total(s0[0] * vx0 + s0[1] * vx1) / mass
    mean_y = total(s0[0] * vy0 + s0[1] * vy1) / mass
    mean_z = total(s1[0] + s1[1]) / mass
    energy = (
        total(
            s0[0] * (vx0 * vx0 + vy0 * vy0) + s0[1] * (vx1 * vx1 + vy1 * vy1) + s2[0] + s2[1]
        )
        / mass
    )
    heat = (energy - (mean_x * mean_x + mean_y * mean_y + mean_z * mean_z)) / 3.0
    variance = 2.0 * math.pi * heat
    rate = rate_scale * mass
    scale = time_step * rate * mass / (variance * jnp.sqrt(variance))
    inverse_heat = -1.0 / (2.0 * heat)
    divisor = 1.0 / (1.0 + time_step * rate)
    flat = [(vx - mean_x) ** 2 + (vy - mean_y) ** 2 for vx, vy in velocities]
    for a in range(M):
        away = (vz[a] - mean_z) ** 2
        for c in range(2):
            maxwell = scale * jnp.exp((flat[c] + away) * inverse_heat)
            change = gain[8 * a : 8 * a + 8, 128 * c : 128 * c + 128]
            out_ref[k, a, c] = (x_ref[k, a, c] + time_step * change + maxwell) * divisor


def kernel(
    g,
    gl,
    gr,
    lk,
    w_forward,
    w_inverse,
    out,
    halo_a,
    halo_b,
    adv,
    cells,
    ready,
    field,
    tables,
    spec,
    gain,
    halo_send,
    halo_recv,
    out_send,
    out_recv,
    back_send,
    back_recv,
    local_sem,
):
    s = lax.axis_index("space")
    j = lax.axis_index("vel")
    count = lax.axis_size("space")
    after = (lax.rem(s + 1, count), j)
    before = (lax.rem(s + count - 1, count), j)
    peers = [lax.rem(j + o, NP) for o in range(NP)]

    barrier = pltpu.get_barrier_semaphore()
    for d in (after, before):
        pl.semaphore_signal(barrier, inc=1, device_id=d, device_id_type=MESH)
    for o in range(1, NP):
        pl.semaphore_signal(barrier, inc=1, device_id=(s, peers[o]), device_id_type=MESH)

    for p in range(4):
        for q in range(M):
            tables[p, q] = jnp.broadcast_to(gl[p : p + 1, 256 * q : 256 * q + 256], (8, 256))
            tables[p + 4, q] = jnp.broadcast_to(gr[p : p + 1, 256 * q : 256 * q + 256], (8, 256))
    for q in range(M):
        tables[8, q] = jnp.broadcast_to(lk[0:1, 256 * q : 256 * q + 256], (8, 256))

    pl.semaphore_wait(barrier, NP + 1)

    def halo_copies(step, source, landing, k):
        low_two, low_one, high_two, high_one = landing
        zs = pl.ds(2 * k, 2)
        pairs = (
            (source.at[zs, :, 1], low_two.at[zs], after),
            (source.at[zs, :, 0, 1], low_one.at[zs], after),
            (source.at[zs, :, 0], high_two.at[zs], before),
            (source.at[zs, :, 1, 0], high_one.at[zs], before),
        )
        return [
            pltpu.make_async_remote_copy(
                src_ref=src,
                dst_ref=dst,
                send_sem=halo_send.at[step, k, i],
                recv_sem=halo_recv.at[step, k, i],
                device_id=d,
                device_id_type=MESH,
            )
            for i, (src, dst, d) in enumerate(pairs)
        ]

    def planes_beside(landing, a_l, c_hi, zs):
        low_two, low_one, high_two, high_one = landing
        if c_hi:
            return low_two[zs, a_l], high_one[zs, a_l][:, None]
        return low_one[zs, a_l][:, None], high_two[zs, a_l]

    def out_copy(k, o):
        return pltpu.make_async_remote_copy(
            src_ref=adv.at[k, peers[o]],
            dst_ref=cells.at[k, pl.ds(2 * j, 2)],
            send_sem=out_send.at[k, o],
            recv_sem=out_recv.at[k, o],
            device_id=(s, peers[o]),
            device_id_type=MESH,
        )

    def place(k, owner):
        return field.at[
            2 * k + lax.rem(lax.div(owner, 2), 2),
            :,
            :,
            lax.div(owner, 4),
            pl.ds(pl.multiple_of(8 * lax.rem(owner, 2), 8), 8),
        ]

    def back_copy(k, o):
        return pltpu.make_async_remote_copy(
            src_ref=ready.at[k, pl.ds(2 * peers[o], 2)],
            dst_ref=place(k, j),
            send_sem=back_send.at[k, o],
            recv_sem=back_recv.at[k, o],
            device_id=(s, peers[o]),
            device_id_type=MESH,
        )

    first = [halo_copies(0, g, halo_a, k) for k in range(CH)]
    for copies in first:
        for copy in copies:
            copy.start()

    outs = [[out_copy(k, o) for o in range(1, NP)] for k in range(CH)]
    own_out = [
        pltpu.make_async_copy(adv.at[k, j], cells.at[k, pl.ds(2 * j, 2)], local_sem.at[0, k])
        for k in range(CH)
    ]
    for k in range(CH):
        for copy in first[k]:
            copy.wait_recv()

        def advance(a_l, c):
            vel_z = jnp.full((1, 128), level(2 * j + a_l), f32)
            for c_hi in range(2):
                vel_x, vel_y = lane_velocities(c_hi)
                low, high = planes_beside(halo_a, a_l, c_hi, pl.ds(2 * k, 2))
                new = moved(
                    g[:, a_l, c_hi], low, high, c_hi == 1, vel_x, vel_y, vel_z, (2 * k, 2 * k + 1)
                )
                for x in range(2):
                    for z in range(2):
                        for h in range(2):
                            adv[k, 4 * x + 2 * z + h, a_l, c_hi] = new[z, x, 8 * h : 8 * h + 8]
            return c

        lax.fori_loop(0, 2, advance, 0)
        for copy in outs[k]:
            copy.start()
        own_out[k].start()

    backs = [[back_copy(k, o) for o in range(1, NP)] for k in range(CH)]
    own_back = [
        pltpu.make_async_copy(ready.at[k, pl.ds(2 * j, 2)], place(k, j), local_sem.at[1, k])
        for k in range(CH)
    ]
    for k in range(CH):
        own_out[k].wait()
        for copy in outs[k]:
            copy.wait_recv()
        relaxed_cells(k, cells, tables, w_forward, w_inverse, spec, gain, ready)
        for copy in backs[k]:
            copy.start()
        own_back[k].start()

    second = [halo_copies(1, field, halo_b, k) for k in range(CH)]
    for k in range(CH):
        own_back[k].wait()
        for copy in backs[k]:
            copy.wait_recv()
        for copy in second[k]:
            copy.start()
    for k in range(CH):
        for copy in second[k]:
            copy.wait_recv()

    def finish(a_l, c):
        vel_z = jnp.full((1, 128), level(2 * j + a_l), f32)
        for c_hi in range(2):
            vel_x, vel_y = lane_velocities(c_hi)
            low, high = planes_beside(halo_b, a_l, c_hi, pl.ds(0, 4))
            out[:, a_l, c_hi] = moved(
                field[:, a_l, c_hi], low, high, c_hi == 1, vel_x, vel_y, vel_z, (0, 1, 2, 3)
            )
        return c

    lax.fori_loop(0, 2, finish, 0)
    for group in (*first, *second, *outs, *backs):
        for copy in group:
            copy.wait_send()


def weights():
    index = np.arange(256)
    phase = (index[:, None] // 16 * (index[None, :] // 16) + index[:, None] % 16 * (index[None, :] % 16)) % 16
    cos, sin = np.cos(phase * (np.pi / 8)), np.sin(phase * (np.pi / 8))

    def held(m):
        m = m.astype(np.float32)
        hi = m.astype(jnp.bfloat16)
        lo = (m - hi.astype(np.float32)).astype(jnp.bfloat16)
        return np.concatenate([hi, hi, lo], axis=0)

    forward = held(np.concatenate([cos, sin], axis=1))
    inverse = held(np.block([[cos, sin], [-sin, cos]]))
    return forward, inverse


def per_device(density, gain_left, gain_right, loss_kernel):
    forward, inverse = weights()
    g = density.reshape(2, 16, 4, 2, 2, 128).transpose(2, 3, 4, 0, 1, 5)
    vmem = pl.BlockSpec(memory_space=pltpu.VMEM)
    dma = pltpu.SemaphoreType.DMA
    landing = (
        pltpu.VMEM((4, 2, 2, 16, 128), f32),
        pltpu.VMEM((4, 2, 16, 128), f32),
        pltpu.VMEM((4, 2, 2, 16, 128), f32),
        pltpu.VMEM((4, 2, 16, 128), f32),
    )
    new = pl.pallas_call(
        kernel,
        out_shape=jax.ShapeDtypeStruct(g.shape, f32),
        in_specs=[vmem] * 6,
        out_specs=vmem,
        scratch_shapes=[
            landing,
            landing,
            pltpu.VMEM((CH, NP, 2, 2, 8, 128), f32),
            pltpu.VMEM((CH, M, 2, 8, 128), f32),
            pltpu.VMEM((CH, M, 2, 8, 128), f32),
            pltpu.VMEM(g.shape, f32),
            pltpu.VMEM((9, M, 8, 256), f32),
            pltpu.VMEM((M, 2, 8, 256), f32),
            pltpu.VMEM((128, 256), f32),
            dma((2, CH, 4)),
            dma((2, CH, 4)),
            dma((CH, NP)),
            dma((CH, NP)),
            dma((CH, NP)),
            dma((CH, NP)),
            dma((2, CH)),
        ],
        compiler_params=pltpu.CompilerParams(
            collective_id=0, has_side_effects=True, vmem_limit_bytes=48 * 1024 * 1024
        ),
    )(g, gain_left, gain_right, loss_kernel.reshape(1, -1), jnp.asarray(forward), jnp.asarray(inverse))
    return new.transpose(3, 4, 0, 1, 2, 5).reshape(density.shape)


def solution(mesh):
    in_specs = (P("space", None, None, "vel"), P(), P(), P())
    out_specs = P("space", None, None, "vel")
    return jax.shard_map(
        per_device, mesh=mesh, in_specs=in_specs, out_specs=out_specs, check_vma=False
    )
```

```python
import math

import jax
import jax.numpy as jnp
import numpy as np
from jax import lax
from jax.experimental import pallas as pl
from jax.experimental.pallas import tpu as pltpu
from jax.sharding import PartitionSpec as P

MESH = pl.DeviceIdType.MESH
M = 16
NP = 8
RUN = 8
CH = 2
courant = 1.0 / 6.0
time_step = 0.25
rate_scale = 0.25
f32 = jnp.float32
bf16 = jnp.bfloat16


def times_root(re, im, k, n, sign):
    k = k % n
    if k == 0:
        return re, im
    if 4 * k == n:
        return (-im, re) if sign > 0 else (im, -re)
    if 2 * k == n:
        return -re, -im
    if 4 * k == 3 * n:
        return (im, -re) if sign > 0 else (-im, re)
    c, s = math.cos(2 * math.pi * k / n), sign * math.sin(2 * math.pi * k / n)
    if 8 * k % n == 0:
        r = math.sqrt(0.5)
        cs, ss = (1 if c > 0 else -1), (1 if s > 0 else -1)
        a = re if cs > 0 else -re
        b = im if ss > 0 else -im
        d = re if ss > 0 else -re
        e = im if cs > 0 else -im
        return (a - b) * r, (d + e) * r
    return re * c - im * s, re * s + im * c


def transform(values, sign):
    n = len(values)
    if n == 1:
        return values
    even = transform(values[0::2], sign)
    odd = transform(values[1::2], sign)
    out = [None] * n
    for k in range(n // 2):
        tr, ti = times_root(*odd[k], k, n, sign)
        er, ei = even[k]
        out[k] = (er + tr, ei + ti)
        out[k + n // 2] = (er - tr, ei - ti)
    return out


def real_transform(values):
    n = len(values)
    if n == 1:
        return [(values[0], None)]
    if n == 2:
        return [(values[0] + values[1], None), (values[0] - values[1], None)]
    even = real_transform(values[0::2])
    odd = real_transform(values[1::2])
    out = [None] * (n // 2 + 1)
    h = n // 2
    for k in range(n // 4 + 1):
        er, ei = even[k]
        o_r, o_i = odd[k]
        if k == 0:
            out[0] = (er + o_r, None)
            out[h] = (er - o_r, None)
        elif k == n // 4:
            out[k] = (er, -o_r)
        else:
            tr, ti = times_root(o_r, o_i, k, n, -1)
            out[k] = (er + tr, ei + ti)
            out[h - k] = (er - tr, ti - ei)
    return out


def minmod(p, q):
    return jnp.minimum(jnp.maximum(p, jnp.minimum(q, 0.0)), jnp.maximum(q, 0.0))


def turned(v, by):
    n = v.shape[-2]
    if by > 0:
        return jnp.concatenate([v[..., n - 1 :, :], v[..., : n - 1, :]], axis=-2)
    return jnp.concatenate([v[..., 1:, :], v[..., :1, :]], axis=-2)


def moved(g, low, high, positive, vel_x, vel_y, vel_z, zs):
    sign = 0.5 if positive else -0.5
    here = g[zs[0] : zs[-1] + 1]
    planes = jnp.concatenate([low, here, high], axis=1)
    d = planes[:, 1:] - planes[:, :-1]
    face = planes[:, 1:4] + sign * minmod(d[:, :-1], d[:, 1:])
    jump_x = face[:, 1:] - face[:, :-1]

    up_y = vel_y > 0.0
    half_y = jnp.where(up_y, 0.5, -0.5)
    d = here - turned(here, 1)
    face = here + half_y * minmod(d, turned(d, -1))
    e = face - turned(face, 1)
    jump_y = jnp.where(up_y, e, turned(e, -1))

    up_z = vel_z > 0.0
    half_z = jnp.where(up_z, 0.5, -0.5)
    d = [g[z] - g[(z + 3) % 4] for z in range(4)]
    face = [g[z] + half_z * minmod(d[z], d[(z + 1) % 4]) for z in range(4)]
    e = [face[z] - face[(z + 3) % 4] for z in range(4)]
    jump_z = jnp.stack([jnp.where(up_z, e[z], e[(z + 1) % 4]) for z in zs])
    return here - courant * (vel_x * jump_x + vel_y * jump_y + vel_z * jump_z)


def lane_velocities(c_hi):
    lane = lax.broadcasted_iota(jnp.int32, (1, 128), 1)
    vel_x = (2.0 * ((lane >> 4) + 8 * c_hi).astype(f32) + 1.0) / M - 1.0
    vel_y = (2.0 * (lane & 15).astype(f32) + 1.0) / M - 1.0
    return vel_x, vel_y


def level(a):
    return (2.0 * a.astype(f32) + 1.0) / M - 1.0


def split(v):
    hi = v.astype(bf16)
    lo = (v - hi.astype(f32)).astype(bf16)
    return hi, lo


def product(v, weights):
    hi, lo = split(v)
    return jnp.dot(
        jnp.concatenate([hi, lo, hi], axis=1), weights, preferred_element_type=f32
    )


def wide(v):
    return jnp.concatenate([v[0], v[1]], axis=1)


def relaxed_cells(k, x_ref, tables, w_forward, w_inverse, spec, gain, out_ref):
    rows = [wide(x_ref[k, a]) * (1.0 / M**3) for a in range(M)]
    modes = real_transform(rows)
    parts = [re for re, _ in modes] + [im for _, im in modes[1:8]]
    both = product(jnp.concatenate(parts, axis=0), w_forward[...])
    both = [both[8 * i : 8 * i + 8] for i in range(16)]
    for q in range(9):
        rc, rs = both[q][:, :256], both[q][:, 256:]
        if q in (0, 8):
            spec[q, 0] = rc
            spec[q, 1] = -rs
            continue
        ic, js = both[q + 8][:, :256], both[q + 8][:, 256:]
        spec[q, 0] = rc + js
        spec[q, 1] = ic - rs
        spec[16 - q, 0] = rc - js
        spec[16 - q, 1] = -ic - rs

    def bent(m):
        values = []
        for q in range(M):
            t = tables[m, q]
            values.append((t * spec[q, 0], t * spec[q, 1]))
        values = transform(values, 1)
        return jnp.concatenate(
            [jnp.concatenate([re, im], axis=1) for re, im in values], axis=0
        )

    loss = product(bent(8), w_inverse[:, :256])
    gain[...] = -(jnp.concatenate([wide(x_ref[k, a]) for a in range(M)], axis=0) * loss)

    def term(p, c):
        both = product(jnp.concatenate([bent(p), bent(p + 4)], axis=0), w_inverse[...])
        left, right = both[:128], both[128:]
        gain[...] += left[:, :256] * right[:, :256] - left[:, 256:] * right[:, 256:]
        return c

    lax.fori_loop(0, 4, term, 0)

    velocities = [lane_velocities(c) for c in range(2)]
    weight = (2.0 / M) ** 3
    vz = [(2.0 * a + 1.0) / M - 1.0 for a in range(M)]
    cells = [x_ref[k, a] for a in range(M)]
    s0 = sum(cells[1:], cells[0])
    s1 = sum((cells[a] * vz[a] for a in range(1, M)), cells[0] * vz[0])
    s2 = sum((cells[a] * (vz[a] * vz[a]) for a in range(1, M)), cells[0] * (vz[0] * vz[0]))

    def total(v):
        return jnp.sum(v, axis=-1, keepdims=True) * weight

    (vx0, vy0), (vx1, vy1) = velocities
    mass = total(s0[0] + s0[1])
    mean_x = total(s0[0] * vx0 + s0[1] * vx1) / mass
    mean_y = total(s0[0] * vy0 + s0[1] * vy1) / mass
    mean_z = total(s1[0] + s1[1]) / mass
    energy = (
        total(
            s0[0] * (vx0 * vx0 + vy0 * vy0) + s0[1] * (vx1 * vx1 + vy1 * vy1) + s2[0] + s2[1]
        )
        / mass
    )
    heat = (energy - (mean_x * mean_x + mean_y * mean_y + mean_z * mean_z)) / 3.0
    variance = 2.0 * math.pi * heat
    rate = rate_scale * mass
    scale = time_step * rate * mass / (variance * jnp.sqrt(variance))
    inverse_heat = -1.0 / (2.0 * heat)
    divisor = 1.0 / (1.0 + time_step * rate)
    flat = [(vx - mean_x) ** 2 + (vy - mean_y) ** 2 for vx, vy in velocities]
    for a in range(M):
        away = (vz[a] - mean_z) ** 2
        for c in range(2):
            maxwell = scale * jnp.exp((flat[c] + away) * inverse_heat)
            change = gain[8 * a : 8 * a + 8, 128 * c : 128 * c + 128]
            out_ref[k, a, c] = (x_ref[k, a, c] + time_step * change + maxwell) * divisor


def kernel(
    density,
    gl_far,
    gr_far,
    lk_far,
    w_forward_far,
    w_inverse_far,
    out,
    raw,
    gl,
    gr,
    lk,
    w_forward,
    w_inverse,
    g,
    halo_a,
    halo_b,
    adv,
    cells,
    ready,
    field,
    tables,
    spec,
    gain,
    halo_send,
    halo_recv,
    out_send,
    out_recv,
    back_send,
    back_recv,
    local_sem,
    load_sem,
    far_send,
    far_recv,
    ack,
):
    s = lax.axis_index("space")
    j = lax.axis_index("vel")
    count = lax.axis_size("space")
    after = (lax.rem(s + 1, count), j)
    before = (lax.rem(s + count - 1, count), j)
    peers = [lax.rem(j + o, NP) for o in range(NP)]

    place_in_run = lax.rem(s, RUN)
    is_first, is_last = place_in_run == 0, place_in_run == RUN - 1
    is_edge = jnp.logical_or(is_first, is_last)
    is_inner = jnp.logical_not(is_edge)
    far_s = jnp.where(is_first, before[0], after[0])

    barrier = pltpu.get_barrier_semaphore()

    def tell(d):
        pl.semaphore_signal(barrier, inc=1, device_id=d, device_id_type=MESH)

    @pl.when(is_edge)
    def _():
        for d in range(NP):
            tell((far_s, d))

    @pl.when(jnp.logical_and(is_inner, place_in_run != RUN - 2))
    def _():
        tell(after)

    @pl.when(jnp.logical_and(is_inner, place_in_run != 1))
    def _():
        tell(before)

    @pl.when(is_first)
    def _():
        tell(after)

    @pl.when(is_last)
    def _():
        tell(before)

    for o in range(1, NP):
        tell((s, peers[o]))

    loads = [
        pltpu.make_async_copy(density, raw, load_sem.at[0]),
        pltpu.make_async_copy(w_forward_far, w_forward, load_sem.at[1]),
        pltpu.make_async_copy(w_inverse_far, w_inverse, load_sem.at[2]),
        pltpu.make_async_copy(gl_far, gl, load_sem.at[3]),
        pltpu.make_async_copy(gr_far, gr, load_sem.at[4]),
        pltpu.make_async_copy(lk_far, lk, load_sem.at[5]),
    ]
    for load in loads:
        load.start()
    loads[0].wait()
    for x in range(2):
        for z in range(4):
            for t in range(4):
                g[z, t // 2, t % 2, x] = raw[x, :, z, 128 * t : 128 * t + 128]
    def halo_copies(step, source, landing, k):
        low, high = landing
        zs = pl.ds(2 * k, 2)
        pairs = (
            (source.at[zs, :, 1], low.at[zs, :, 1], after),
            (source.at[zs, :, 0, 1], low.at[zs, :, 0, 1], after),
            (source.at[zs, :, 0], high.at[zs, :, 0], before),
            (source.at[zs, :, 1, 0], high.at[zs, :, 1, 0], before),
        )
        return [
            pltpu.make_async_remote_copy(
                src_ref=src,
                dst_ref=dst,
                send_sem=halo_send.at[step, k, i],
                recv_sem=halo_recv.at[step, k, i],
                device_id=d,
                device_id_type=MESH,
            )
            for i, (src, dst, d) in enumerate(pairs)
        ]

    def planes_beside(landing, a_l, c_hi, zs):
        low, high = landing
        if c_hi:
            return low[zs, a_l, 1], high[zs, a_l, 1, 0:1]
        return low[zs, a_l, 0, 1:2], high[zs, a_l, 0]

    def out_copy(k, o):
        return pltpu.make_async_remote_copy(
            src_ref=adv.at[k, peers[o]],
            dst_ref=cells.at[k, pl.ds(2 * j, 2)],
            send_sem=out_send.at[k, o],
            recv_sem=out_recv.at[k, o],
            device_id=(s, peers[o]),
            device_id_type=MESH,
        )

    def place(k, owner):
        return field.at[
            2 * k + lax.rem(lax.div(owner, 2), 2),
            :,
            :,
            lax.div(owner, 4),
            pl.ds(pl.multiple_of(8 * lax.rem(owner, 2), 8), 8),
        ]

    def back_copy(k, o):
        return pltpu.make_async_remote_copy(
            src_ref=ready.at[k, pl.ds(2 * peers[o], 2)],
            dst_ref=place(k, j),
            send_sem=back_send.at[k, o],
            recv_sem=back_recv.at[k, o],
            device_id=(s, peers[o]),
            device_id_type=MESH,
        )

    def far_copy(k, owner, d, sem, side, both):
        low, high = halo_b
        x = lax.div(owner, 4) if not isinstance(owner, int) else owner // 4
        z = 2 * k + (lax.rem(lax.div(owner, 2), 2) if not isinstance(owner, int) else owner // 2 % 2)
        odd = lax.rem(owner, 2) if not isinstance(owner, int) else owner % 2
        ys = pl.ds(8 * odd if isinstance(owner, int) else pl.multiple_of(8 * odd, 8), 8)
        there = low if side else high
        if both:
            src, dst = ready.at[k, 2 * d : 2 * d + 2], there.at[z, :, :, x, ys]
        else:
            src, dst = ready.at[k, 2 * d : 2 * d + 2, side], there.at[z, :, side, x, ys]
        return pltpu.make_async_remote_copy(
            src_ref=src,
            dst_ref=dst,
            send_sem=far_send.at[k, d],
            recv_sem=far_recv.at[k, sem],
            device_id=(far_s, d),
            device_id_type=MESH,
        )

    def each_far(act, k):
        for side, here in ((1, is_last), (0, is_first)):
            for x in range(2):

                @pl.when(jnp.logical_and(here, lax.div(j, 4) == x))
                def _():
                    for d in range(NP):
                        act(far_copy(k, j, d, j, side, x == side))

    def await_far(k):
        for side, here in ((1, is_first), (0, is_last)):

            @pl.when(here)
            def _():
                for owner in range(NP):
                    far_copy(k, owner, 0, owner, side, owner // 4 == side).wait_recv()

    first = [halo_copies(0, g, halo_a, k) for k in range(CH)]

    def start(copies):
        for copy in copies:
            copy.start()

    @pl.when(is_inner)
    def _():
        pl.semaphore_wait(barrier, NP + 1)

    @pl.when(place_in_run == 1)
    def _():
        pl.semaphore_signal(ack, inc=1, device_id=before, device_id_type=MESH)

    @pl.when(place_in_run == RUN - 2)
    def _():
        pl.semaphore_signal(ack, inc=1, device_id=after, device_id_type=MESH)

    @pl.when(is_edge)
    def _():
        pl.semaphore_wait(ack, 1)

    def start_near(copies):
        pl.when(jnp.logical_not(is_last))(lambda: start(copies[:2]))
        pl.when(jnp.logical_not(is_first))(lambda: start(copies[2:]))

    for k in range(CH):
        start_near(first[k])

    @pl.when(is_edge)
    def _():
        pl.semaphore_wait(barrier, 2 * NP - 1)

    for k in range(CH):
        pl.when(is_last)(lambda k=k: start(first[k][:2]))
        pl.when(is_first)(lambda k=k: start(first[k][2:]))

    for load in loads[1:]:
        load.wait()
    for p in range(4):
        for q in range(M):
            tables[p, q] = jnp.broadcast_to(gl[p : p + 1, 256 * q : 256 * q + 256], (8, 256))
            tables[p + 4, q] = jnp.broadcast_to(gr[p : p + 1, 256 * q : 256 * q + 256], (8, 256))
    for q in range(M):
        tables[8, q] = jnp.broadcast_to(lk[0:1, 256 * q : 256 * q + 256], (8, 256))

    outs = [[out_copy(k, o) for o in range(1, NP)] for k in range(CH)]
    own_out = [
        pltpu.make_async_copy(adv.at[k, j], cells.at[k, pl.ds(2 * j, 2)], local_sem.at[0, k])
        for k in range(CH)
    ]
    for k in range(CH):
        for copy in first[k]:
            copy.wait_recv()

        def advance(a_l, c):
            vel_z = jnp.full((1, 128), level(2 * j + a_l), f32)
            for c_hi in range(2):
                vel_x, vel_y = lane_velocities(c_hi)
                low, high = planes_beside(halo_a, a_l, c_hi, pl.ds(2 * k, 2))
                new = moved(
                    g[:, a_l, c_hi], low, high, c_hi == 1, vel_x, vel_y, vel_z, (2 * k, 2 * k + 1)
                )
                for x in range(2):
                    for z in range(2):
                        for h in range(2):
                            adv[k, 4 * x + 2 * z + h, a_l, c_hi] = new[z, x, 8 * h : 8 * h + 8]
            return c

        lax.fori_loop(0, 2, advance, 0)
        for copy in outs[k]:
            copy.start()
        own_out[k].start()

    backs = [[back_copy(k, o) for o in range(1, NP)] for k in range(CH)]
    own_back = [
        pltpu.make_async_copy(ready.at[k, pl.ds(2 * j, 2)], place(k, j), local_sem.at[1, k])
        for k in range(CH)
    ]
    for k in range(CH):
        own_out[k].wait()
        for copy in outs[k]:
            copy.wait_recv()
        relaxed_cells(k, cells, tables, w_forward, w_inverse, spec, gain, ready)
        each_far(lambda copy: copy.start(), k)
        for copy in backs[k]:
            copy.start()
        own_back[k].start()

    second = [halo_copies(1, field, halo_b, k) for k in range(CH)]
    for k in range(CH):
        own_back[k].wait()
        for copy in backs[k]:
            copy.wait_recv()
        start_near(second[k])
    for k in range(CH):
        pl.when(jnp.logical_not(is_first))(lambda k=k: [copy.wait_recv() for copy in second[k][:2]] and None)
        pl.when(jnp.logical_not(is_last))(lambda k=k: [copy.wait_recv() for copy in second[k][2:]] and None)
        await_far(k)

    def finish(a_l, c):
        vel_z = jnp.full((1, 128), level(2 * j + a_l), f32)
        for c_hi in range(2):
            vel_x, vel_y = lane_velocities(c_hi)
            low, high = planes_beside(halo_b, a_l, c_hi, pl.ds(0, 4))
            out[:, a_l, c_hi] = moved(
                field[:, a_l, c_hi], low, high, c_hi == 1, vel_x, vel_y, vel_z, (0, 1, 2, 3)
            )
        return c

    lax.fori_loop(0, 2, finish, 0)
    for group in (*first, *outs, *backs):
        for copy in group:
            copy.wait_send()
    for k in range(CH):
        pl.when(jnp.logical_not(is_last))(lambda k=k: [copy.wait_send() for copy in second[k][:2]] and None)
        pl.when(jnp.logical_not(is_first))(lambda k=k: [copy.wait_send() for copy in second[k][2:]] and None)
        each_far(lambda copy: copy.wait_send(), k)


def weights():
    index = np.arange(256)
    phase = (index[:, None] // 16 * (index[None, :] // 16) + index[:, None] % 16 * (index[None, :] % 16)) % 16
    cos, sin = np.cos(phase * (np.pi / 8)), np.sin(phase * (np.pi / 8))

    def held(m):
        m = m.astype(np.float32)
        hi = m.astype(jnp.bfloat16)
        lo = (m - hi.astype(np.float32)).astype(jnp.bfloat16)
        return np.concatenate([hi, hi, lo], axis=0)

    forward = held(np.concatenate([cos, sin], axis=1))
    inverse = held(np.block([[cos, sin], [-sin, cos]]))
    return forward, inverse


def per_device(density, gain_left, gain_right, loss_kernel):
    forward, inverse = weights()
    held = (4, 2, 2, 2, 16, 128)
    far = pl.BlockSpec(memory_space=pltpu.HBM)
    vmem = pl.BlockSpec(memory_space=pltpu.VMEM)
    dma = pltpu.SemaphoreType.DMA
    landing = (pltpu.VMEM(held, f32), pltpu.VMEM(held, f32))
    new = pl.pallas_call(
        kernel,
        out_shape=jax.ShapeDtypeStruct(held, f32),
        in_specs=[far] * 6,
        out_specs=vmem,
        scratch_shapes=[
            pltpu.VMEM(density.shape, f32),
            pltpu.VMEM(gain_left.shape, f32),
            pltpu.VMEM(gain_right.shape, f32),
            pltpu.VMEM((1, loss_kernel.shape[0]), f32),
            pltpu.VMEM(forward.shape, bf16),
            pltpu.VMEM(inverse.shape, bf16),
            pltpu.VMEM(held, f32),
            landing,
            landing,
            pltpu.VMEM((CH, NP, 2, 2, 8, 128), f32),
            pltpu.VMEM((CH, M, 2, 8, 128), f32),
            pltpu.VMEM((CH, M, 2, 8, 128), f32),
            pltpu.VMEM(held, f32),
            pltpu.VMEM((9, M, 8, 256), f32),
            pltpu.VMEM((M, 2, 8, 256), f32),
            pltpu.VMEM((128, 256), f32),
            dma((2, CH, 4)),
            dma((2, CH, 4)),
            dma((CH, NP)),
            dma((CH, NP)),
            dma((CH, NP)),
            dma((CH, NP)),
            dma((2, CH)),
            dma((6,)),
            dma((CH, NP)),
            dma((CH, NP)),
            pltpu.SemaphoreType.REGULAR,
        ],
        compiler_params=pltpu.CompilerParams(
            collective_id=0, has_side_effects=True, vmem_limit_bytes=63 * 1024 * 1024
        ),
    )(density, gain_left, gain_right, loss_kernel.reshape(1, -1), jnp.asarray(forward), jnp.asarray(inverse))
    return new.transpose(3, 4, 0, 1, 2, 5).reshape(density.shape)


def solution(mesh):
    in_specs = (P("space", None, None, "vel"), P(), P(), P())
    out_specs = P("space", None, None, "vel")
    return jax.shard_map(
        per_device, mesh=mesh, in_specs=in_specs, out_specs=out_specs, check_vma=False
    )
```

```python
import math

import jax
import jax.numpy as jnp
import numpy as np
from jax import lax
from jax.experimental import pallas as pl
from jax.experimental.pallas import tpu as pltpu
from jax.sharding import PartitionSpec as P

MESH = pl.DeviceIdType.MESH
M = 16
NP = 8
RUN = 8
CH = 2
courant = 1.0 / 6.0
time_step = 0.25
rate_scale = 0.25
f32 = jnp.float32
bf16 = jnp.bfloat16


def times_root(re, im, k, n, sign):
    k = k % n
    if k == 0:
        return re, im
    if 4 * k == n:
        return (-im, re) if sign > 0 else (im, -re)
    if 2 * k == n:
        return -re, -im
    if 4 * k == 3 * n:
        return (im, -re) if sign > 0 else (-im, re)
    c, s = math.cos(2 * math.pi * k / n), sign * math.sin(2 * math.pi * k / n)
    if 8 * k % n == 0:
        r = math.sqrt(0.5)
        cs, ss = (1 if c > 0 else -1), (1 if s > 0 else -1)
        a = re if cs > 0 else -re
        b = im if ss > 0 else -im
        d = re if ss > 0 else -re
        e = im if cs > 0 else -im
        return (a - b) * r, (d + e) * r
    return re * c - im * s, re * s + im * c


def transform(values, sign):
    n = len(values)
    if n == 1:
        return values
    even = transform(values[0::2], sign)
    odd = transform(values[1::2], sign)
    out = [None] * n
    for k in range(n // 2):
        tr, ti = times_root(*odd[k], k, n, sign)
        er, ei = even[k]
        out[k] = (er + tr, ei + ti)
        out[k + n // 2] = (er - tr, ei - ti)
    return out


def real_transform(values):
    n = len(values)
    if n == 1:
        return [(values[0], None)]
    if n == 2:
        return [(values[0] + values[1], None), (values[0] - values[1], None)]
    even = real_transform(values[0::2])
    odd = real_transform(values[1::2])
    out = [None] * (n // 2 + 1)
    h = n // 2
    for k in range(n // 4 + 1):
        er, ei = even[k]
        o_r, o_i = odd[k]
        if k == 0:
            out[0] = (er + o_r, None)
            out[h] = (er - o_r, None)
        elif k == n // 4:
            out[k] = (er, -o_r)
        else:
            tr, ti = times_root(o_r, o_i, k, n, -1)
            out[k] = (er + tr, ei + ti)
            out[h - k] = (er - tr, ti - ei)
    return out


def minmod(p, q):
    return jnp.minimum(jnp.maximum(p, jnp.minimum(q, 0.0)), jnp.maximum(q, 0.0))


def turned(v, by):
    n = v.shape[-2]
    if by > 0:
        return jnp.concatenate([v[..., n - 1 :, :], v[..., : n - 1, :]], axis=-2)
    return jnp.concatenate([v[..., 1:, :], v[..., :1, :]], axis=-2)


def moved(g, low, high, positive, vel_x, vel_y, vel_z, zs):
    sign = 0.5 if positive else -0.5
    here = g[zs[0] : zs[-1] + 1]
    planes = jnp.concatenate([low, here, high], axis=1)
    d = planes[:, 1:] - planes[:, :-1]
    face = planes[:, 1:4] + sign * minmod(d[:, :-1], d[:, 1:])
    jump_x = face[:, 1:] - face[:, :-1]

    up_y = vel_y > 0.0
    half_y = jnp.where(up_y, 0.5, -0.5)
    d = here - turned(here, 1)
    face = here + half_y * minmod(d, turned(d, -1))
    e = face - turned(face, 1)
    jump_y = jnp.where(up_y, e, turned(e, -1))

    up_z = vel_z > 0.0
    half_z = jnp.where(up_z, 0.5, -0.5)
    d = [g[z] - g[(z + 3) % 4] for z in range(4)]
    face = [g[z] + half_z * minmod(d[z], d[(z + 1) % 4]) for z in range(4)]
    e = [face[z] - face[(z + 3) % 4] for z in range(4)]
    jump_z = jnp.stack([jnp.where(up_z, e[z], e[(z + 1) % 4]) for z in zs])
    return here - courant * (vel_x * jump_x + vel_y * jump_y + vel_z * jump_z)


def lane_velocities(c_hi):
    lane = lax.broadcasted_iota(jnp.int32, (1, 128), 1)
    vel_x = (2.0 * ((lane >> 4) + 8 * c_hi).astype(f32) + 1.0) / M - 1.0
    vel_y = (2.0 * (lane & 15).astype(f32) + 1.0) / M - 1.0
    return vel_x, vel_y


def level(a):
    return (2.0 * a.astype(f32) + 1.0) / M - 1.0


def split(v):
    hi = v.astype(bf16)
    lo = (v - hi.astype(f32)).astype(bf16)
    return hi, lo


def product(v, weights):
    hi, lo = split(v)
    return jnp.dot(
        jnp.concatenate([hi, lo, hi], axis=1), weights, preferred_element_type=f32
    )


def wide(v):
    return jnp.concatenate([v[0], v[1]], axis=1)


def relaxed_cells(k, x_ref, tables, w_forward, w_inverse, spec, gain, out_ref):
    rows = [wide(x_ref[k, a]) * (1.0 / M**3) for a in range(M)]
    modes = real_transform(rows)
    parts = [re for re, _ in modes] + [im for _, im in modes[1:8]]
    both = product(jnp.concatenate(parts, axis=0), w_forward[...])
    both = [both[8 * i : 8 * i + 8] for i in range(16)]
    for q in range(9):
        rc, rs = both[q][:, :256], both[q][:, 256:]
        if q in (0, 8):
            spec[q, 0] = rc
            spec[q, 1] = -rs
            continue
        ic, js = both[q + 8][:, :256], both[q + 8][:, 256:]
        spec[q, 0] = rc + js
        spec[q, 1] = ic - rs
        spec[16 - q, 0] = rc - js
        spec[16 - q, 1] = -ic - rs

    def bent(m):
        values = []
        for q in range(M):
            t = tables[m, q]
            values.append((t * spec[q, 0], t * spec[q, 1]))
        values = transform(values, 1)
        return jnp.concatenate(
            [jnp.concatenate([re, im], axis=1) for re, im in values], axis=0
        )

    loss = product(bent(8), w_inverse[:, :256])
    gain[...] = -(jnp.concatenate([wide(x_ref[k, a]) for a in range(M)], axis=0) * loss)

    def term(p, c):
        both = product(jnp.concatenate([bent(p), bent(p + 4)], axis=0), w_inverse[...])
        left, right = both[:128], both[128:]
        gain[...] += left[:, :256] * right[:, :256] - left[:, 256:] * right[:, 256:]
        return c

    for p in range(4):
        term(p, 0)

    velocities = [lane_velocities(c) for c in range(2)]
    weight = (2.0 / M) ** 3
    vz = [(2.0 * a + 1.0) / M - 1.0 for a in range(M)]
    cells = [x_ref[k, a] for a in range(M)]
    s0 = sum(cells[1:], cells[0])
    s1 = sum((cells[a] * vz[a] for a in range(1, M)), cells[0] * vz[0])
    s2 = sum((cells[a] * (vz[a] * vz[a]) for a in range(1, M)), cells[0] * (vz[0] * vz[0]))

    def total(v):
        return jnp.sum(v, axis=-1, keepdims=True) * weight

    (vx0, vy0), (vx1, vy1) = velocities
    mass = total(s0[0] + s0[1])
    mean_x = total(s0[0] * vx0 + s0[1] * vx1) / mass
    mean_y = total(s0[0] * vy0 + s0[1] * vy1) / mass
    mean_z = total(s1[0] + s1[1]) / mass
    energy = (
        total(
            s0[0] * (vx0 * vx0 + vy0 * vy0) + s0[1] * (vx1 * vx1 + vy1 * vy1) + s2[0] + s2[1]
        )
        / mass
    )
    heat = (energy - (mean_x * mean_x + mean_y * mean_y + mean_z * mean_z)) / 3.0
    variance = 2.0 * math.pi * heat
    rate = rate_scale * mass
    scale = time_step * rate * mass / (variance * jnp.sqrt(variance))
    inverse_heat = -1.0 / (2.0 * heat)
    divisor = 1.0 / (1.0 + time_step * rate)
    flat = [(vx - mean_x) ** 2 + (vy - mean_y) ** 2 for vx, vy in velocities]
    for a in range(M):
        away = (vz[a] - mean_z) ** 2
        for c in range(2):
            maxwell = scale * jnp.exp((flat[c] + away) * inverse_heat)
            change = gain[8 * a : 8 * a + 8, 128 * c : 128 * c + 128]
            out_ref[k, a, c] = (x_ref[k, a, c] + time_step * change + maxwell) * divisor


def kernel(
    density,
    gl_far,
    gr_far,
    lk_far,
    w_forward_far,
    w_inverse_far,
    out,
    raw,
    gl,
    gr,
    lk,
    w_forward,
    w_inverse,
    g,
    halo_a,
    halo_b,
    adv,
    cells,
    ready,
    field,
    tables,
    spec,
    gain,
    halo_send,
    halo_recv,
    out_send,
    out_recv,
    back_send,
    back_recv,
    local_sem,
    load_sem,
    far_send,
    far_recv,
    ack,
):
    s = lax.axis_index("space")
    j = lax.axis_index("vel")
    count = lax.axis_size("space")
    after = (lax.rem(s + 1, count), j)
    before = (lax.rem(s + count - 1, count), j)
    order = [sorted((d for d in range(NP) if d != i), key=lambda d: -abs(d - i)) for i in range(NP)]
    peers = []
    for n in range(NP - 1):
        d = jnp.int32(order[0][n])
        for i in range(1, NP):
            d = jnp.where(j == i, order[i][n], d)
        peers.append(d)

    place_in_run = lax.rem(s, RUN)
    is_first, is_last = place_in_run == 0, place_in_run == RUN - 1
    is_edge = jnp.logical_or(is_first, is_last)
    is_inner = jnp.logical_not(is_edge)
    far_s = jnp.where(is_first, before[0], after[0])

    barrier = pltpu.get_barrier_semaphore()

    def tell(d):
        pl.semaphore_signal(barrier, inc=1, device_id=d, device_id_type=MESH)

    @pl.when(is_edge)
    def _():
        tell((far_s, j))

    @pl.when(jnp.logical_and(is_inner, place_in_run != RUN - 2))
    def _():
        tell(after)

    @pl.when(jnp.logical_and(is_inner, place_in_run != 1))
    def _():
        tell(before)

    @pl.when(is_first)
    def _():
        tell(after)

    @pl.when(is_last)
    def _():
        tell(before)

    for d in peers:
        tell((s, d))

    loads = [
        pltpu.make_async_copy(density, raw, load_sem.at[0]),
        pltpu.make_async_copy(w_forward_far, w_forward, load_sem.at[1]),
        pltpu.make_async_copy(w_inverse_far, w_inverse, load_sem.at[2]),
        pltpu.make_async_copy(gl_far, gl, load_sem.at[3]),
        pltpu.make_async_copy(gr_far, gr, load_sem.at[4]),
        pltpu.make_async_copy(lk_far, lk, load_sem.at[5]),
    ]
    for load in loads:
        load.start()
    loads[0].wait()
    for x in range(2):
        for z in range(4):
            for t in range(4):
                g[z, t // 2, t % 2, x] = raw[x, :, z, 128 * t : 128 * t + 128]
    def halo_copies(step, source, landing, k):
        low, high = landing
        zs = pl.ds(2 * k, 2)
        pairs = (
            (source.at[zs, :, 1], low.at[zs, :, 1], after),
            (source.at[zs, :, 0, 1], low.at[zs, :, 0, 1], after),
            (source.at[zs, :, 0], high.at[zs, :, 0], before),
            (source.at[zs, :, 1, 0], high.at[zs, :, 1, 0], before),
        )
        return [
            pltpu.make_async_remote_copy(
                src_ref=src,
                dst_ref=dst,
                send_sem=halo_send.at[step, k, i],
                recv_sem=halo_recv.at[step, k, i],
                device_id=d,
                device_id_type=MESH,
            )
            for i, (src, dst, d) in enumerate(pairs)
        ]

    def planes_beside(landing, a_l, c_hi, zs):
        low, high = landing
        if c_hi:
            return low[zs, a_l, 1], high[zs, a_l, 1, 0:1]
        return low[zs, a_l, 0, 1:2], high[zs, a_l, 0]

    def out_copy(k, d):
        return pltpu.make_async_remote_copy(
            src_ref=adv.at[k, d],
            dst_ref=cells.at[k, pl.ds(2 * j, 2)],
            send_sem=out_send.at[k, d],
            recv_sem=out_recv.at[k, j],
            device_id=(s, d),
            device_id_type=MESH,
        )

    def arrival(k, d, dst, sem):
        return pltpu.make_async_remote_copy(
            src_ref=adv.at[k, d],
            dst_ref=dst,
            send_sem=out_send.at[k, d],
            recv_sem=sem.at[k, d],
            device_id=(s, d),
            device_id_type=MESH,
        )

    def place(k, owner):
        return field.at[
            2 * k + lax.rem(lax.div(owner, 2), 2),
            :,
            :,
            lax.div(owner, 4),
            pl.ds(pl.multiple_of(8 * lax.rem(owner, 2), 8), 8),
        ]

    def back_copy(k, d):
        return pltpu.make_async_remote_copy(
            src_ref=ready.at[k, pl.ds(2 * d, 2)],
            dst_ref=place(k, j),
            send_sem=back_send.at[k, d],
            recv_sem=back_recv.at[k, j],
            device_id=(s, d),
            device_id_type=MESH,
        )

    def far_copy(k, owner, d, sem, side, both):
        low, high = halo_b
        x = lax.div(owner, 4) if not isinstance(owner, int) else owner // 4
        z = 2 * k + (lax.rem(lax.div(owner, 2), 2) if not isinstance(owner, int) else owner // 2 % 2)
        odd = lax.rem(owner, 2) if not isinstance(owner, int) else owner % 2
        ys = pl.ds(8 * odd if isinstance(owner, int) else pl.multiple_of(8 * odd, 8), 8)
        there = low if side else high
        if both:
            src, dst = ready.at[k, pl.ds(2 * d, 2)], there.at[z, :, :, x, ys]
        else:
            src, dst = ready.at[k, pl.ds(2 * d, 2), side], there.at[z, :, side, x, ys]
        return pltpu.make_async_remote_copy(
            src_ref=src,
            dst_ref=dst,
            send_sem=far_send.at[k, d],
            recv_sem=far_recv.at[k, sem],
            device_id=(far_s, d),
            device_id_type=MESH,
        )

    def each_far(act, k):
        for side, here in ((1, is_last), (0, is_first)):
            for x in range(2):

                @pl.when(jnp.logical_and(here, lax.div(j, 4) == x))
                def _():
                    for d in (j, *reversed(peers)):
                        act(far_copy(k, j, d, j, side, x == side))

    def await_far(k):
        for side, here in ((1, is_first), (0, is_last)):

            @pl.when(here)
            def _():
                for owner in range(NP):
                    far_copy(k, owner, 0, owner, side, owner // 4 == side).wait_recv()

    first = [halo_copies(0, g, halo_a, k) for k in range(CH)]

    def start(copies):
        for copy in copies:
            copy.start()

    @pl.when(is_inner)
    def _():
        pl.semaphore_wait(barrier, NP + 1)

    @pl.when(place_in_run == 1)
    def _():
        pl.semaphore_signal(ack, inc=1, device_id=before, device_id_type=MESH)

    @pl.when(place_in_run == RUN - 2)
    def _():
        pl.semaphore_signal(ack, inc=1, device_id=after, device_id_type=MESH)

    @pl.when(is_edge)
    def _():
        pl.semaphore_wait(ack, 1)

    def start_near(copies):
        pl.when(jnp.logical_not(is_last))(lambda: start(copies[:2]))
        pl.when(jnp.logical_not(is_first))(lambda: start(copies[2:]))

    for k in range(CH):
        start_near(first[k])

    @pl.when(is_edge)
    def _():
        pl.semaphore_wait(barrier, NP)

    def start_far(copies):
        pl.when(is_last)(lambda: start(copies[:2]))
        pl.when(is_first)(lambda: start(copies[2:]))

    start_far(first[0])
    for load in loads[1:]:
        load.wait()
    for p in range(4):
        for q in range(M):
            tables[p, q] = jnp.broadcast_to(gl[p : p + 1, 256 * q : 256 * q + 256], (8, 256))
            tables[p + 4, q] = jnp.broadcast_to(gr[p : p + 1, 256 * q : 256 * q + 256], (8, 256))
    for q in range(M):
        tables[8, q] = jnp.broadcast_to(lk[0:1, 256 * q : 256 * q + 256], (8, 256))
    start_far(first[1])

    outs = [[out_copy(k, d) for d in peers] for k in range(CH)]
    own_out = [
        pltpu.make_async_copy(adv.at[k, j], cells.at[k, pl.ds(2 * j, 2)], local_sem.at[0, k])
        for k in range(CH)
    ]
    for k in range(CH):
        for copy in first[k]:
            copy.wait_recv()

        def advance(a_l, c):
            vel_z = jnp.full((1, 128), level(2 * j + a_l), f32)
            for c_hi in range(2):
                vel_x, vel_y = lane_velocities(c_hi)
                low, high = planes_beside(halo_a, a_l, c_hi, pl.ds(2 * k, 2))
                new = moved(
                    g[:, a_l, c_hi], low, high, c_hi == 1, vel_x, vel_y, vel_z, (2 * k, 2 * k + 1)
                )
                for x in range(2):
                    for z in range(2):
                        for h in range(2):
                            adv[k, 4 * x + 2 * z + h, a_l, c_hi] = new[z, x, 8 * h : 8 * h + 8]
            return c

        lax.fori_loop(0, 2, advance, 0)
        for copy in outs[k]:
            copy.start()
        own_out[k].start()

    backs = [[back_copy(k, d) for d in peers] for k in range(CH)]
    own_back = [
        pltpu.make_async_copy(ready.at[k, pl.ds(2 * j, 2)], place(k, j), local_sem.at[1, k])
        for k in range(CH)
    ]
    for k in range(CH):
        own_out[k].wait()
        for d in peers:
            arrival(k, d, cells.at[k, pl.ds(2 * d, 2)], out_recv).wait_recv()
        relaxed_cells(k, cells, tables, w_forward, w_inverse, spec, gain, ready)
        each_far(lambda copy: copy.start(), k)
        for copy in backs[k]:
            copy.start()
        own_back[k].start()

    second = [halo_copies(1, field, halo_b, k) for k in range(CH)]
    for k in range(CH):
        own_back[k].wait()
        for d in peers:
            arrival(k, d, place(k, d), back_recv).wait_recv()
        start_near(second[k])
    for k in range(CH):
        pl.when(jnp.logical_not(is_first))(lambda k=k: [copy.wait_recv() for copy in second[k][:2]] and None)
        pl.when(jnp.logical_not(is_last))(lambda k=k: [copy.wait_recv() for copy in second[k][2:]] and None)
        await_far(k)

    def finish(a_l):
        vel_z = jnp.full((1, 128), level(2 * j + a_l), f32)
        for c_hi in range(2):
            vel_x, vel_y = lane_velocities(c_hi)
            low, high = planes_beside(halo_b, a_l, c_hi, pl.ds(0, 4))
            new = moved(
                field[:, a_l, c_hi], low, high, c_hi == 1, vel_x, vel_y, vel_z, (0, 1, 2, 3)
            )
            lanes = slice(128 * (2 * a_l + c_hi), 128 * (2 * a_l + c_hi + 1))
            for x in range(2):
                for z in range(4):
                    out[x, :, z, lanes] = new[z, x]

    finish(0)
    finish(1)
    for group in (*first, *outs, *backs):
        for copy in group:
            copy.wait_send()
    for k in range(CH):
        pl.when(jnp.logical_not(is_last))(lambda k=k: [copy.wait_send() for copy in second[k][:2]] and None)
        pl.when(jnp.logical_not(is_first))(lambda k=k: [copy.wait_send() for copy in second[k][2:]] and None)
        each_far(lambda copy: copy.wait_send(), k)


def weights():
    index = np.arange(256)
    phase = (index[:, None] // 16 * (index[None, :] // 16) + index[:, None] % 16 * (index[None, :] % 16)) % 16
    cos, sin = np.cos(phase * (np.pi / 8)), np.sin(phase * (np.pi / 8))

    def held(m):
        m = m.astype(np.float32)
        hi = m.astype(jnp.bfloat16)
        lo = (m - hi.astype(np.float32)).astype(jnp.bfloat16)
        return np.concatenate([hi, hi, lo], axis=0)

    forward = held(np.concatenate([cos, sin], axis=1))
    inverse = held(np.block([[cos, sin], [-sin, cos]]))
    return forward, inverse


def per_device(density, gain_left, gain_right, loss_kernel):
    forward, inverse = weights()
    held = (4, 2, 2, 2, 16, 128)
    far = pl.BlockSpec(memory_space=pltpu.HBM)
    vmem = pl.BlockSpec(memory_space=pltpu.VMEM)
    dma = pltpu.SemaphoreType.DMA
    landing = (pltpu.VMEM(held, f32), pltpu.VMEM(held, f32))
    return pl.pallas_call(
        kernel,
        out_shape=jax.ShapeDtypeStruct(density.shape, f32),
        in_specs=[far] * 6,
        out_specs=vmem,
        scratch_shapes=[
            pltpu.VMEM(density.shape, f32),
            pltpu.VMEM(gain_left.shape, f32),
            pltpu.VMEM(gain_right.shape, f32),
            pltpu.VMEM((1, loss_kernel.shape[0]), f32),
            pltpu.VMEM(forward.shape, bf16),
            pltpu.VMEM(inverse.shape, bf16),
            pltpu.VMEM(held, f32),
            landing,
            landing,
            pltpu.VMEM((CH, NP, 2, 2, 8, 128), f32),
            pltpu.VMEM((CH, M, 2, 8, 128), f32),
            pltpu.VMEM((CH, M, 2, 8, 128), f32),
            pltpu.VMEM(held, f32),
            pltpu.VMEM((9, M, 8, 256), f32),
            pltpu.VMEM((M, 2, 8, 256), f32),
            pltpu.VMEM((128, 256), f32),
            dma((2, CH, 4)),
            dma((2, CH, 4)),
            dma((CH, NP)),
            dma((CH, NP)),
            dma((CH, NP)),
            dma((CH, NP)),
            dma((2, CH)),
            dma((6,)),
            dma((CH, NP)),
            dma((CH, NP)),
            pltpu.SemaphoreType.REGULAR,
        ],
        compiler_params=pltpu.CompilerParams(
            collective_id=0, has_side_effects=True, vmem_limit_bytes=63 * 1024 * 1024
        ),
    )(density, gain_left, gain_right, loss_kernel.reshape(1, -1), jnp.asarray(forward), jnp.asarray(inverse))


def solution(mesh):
    in_specs = (P("space", None, None, "vel"), P(), P(), P())
    out_specs = P("space", None, None, "vel")
    return jax.shard_map(
        per_device, mesh=mesh, in_specs=in_specs, out_specs=out_specs, check_vma=False
    )
```

```python
import math

import jax
import jax.numpy as jnp
import numpy as np
from jax import lax
from jax.experimental import pallas as pl
from jax.experimental.pallas import tpu as pltpu
from jax.sharding import PartitionSpec as P

MESH = pl.DeviceIdType.MESH
M = 16
NP = 8
RUN = 8
CH = 2
courant = 1.0 / 6.0
time_step = 0.25
rate_scale = 0.25
f32 = jnp.float32
bf16 = jnp.bfloat16


def times_root(re, im, k, n, sign):
    k = k % n
    if k == 0:
        return re, im
    if 4 * k == n:
        return (-im, re) if sign > 0 else (im, -re)
    if 2 * k == n:
        return -re, -im
    if 4 * k == 3 * n:
        return (im, -re) if sign > 0 else (-im, re)
    c, s = math.cos(2 * math.pi * k / n), sign * math.sin(2 * math.pi * k / n)
    if 8 * k % n == 0:
        r = math.sqrt(0.5)
        cs, ss = (1 if c > 0 else -1), (1 if s > 0 else -1)
        a = re if cs > 0 else -re
        b = im if ss > 0 else -im
        d = re if ss > 0 else -re
        e = im if cs > 0 else -im
        return (a - b) * r, (d + e) * r
    return re * c - im * s, re * s + im * c


def transform(values, sign):
    n = len(values)
    if n == 1:
        return values
    even = transform(values[0::2], sign)
    odd = transform(values[1::2], sign)
    out = [None] * n
    for k in range(n // 2):
        tr, ti = times_root(*odd[k], k, n, sign)
        er, ei = even[k]
        out[k] = (er + tr, ei + ti)
        out[k + n // 2] = (er - tr, ei - ti)
    return out


def real_transform(values):
    n = len(values)
    if n == 1:
        return [(values[0], None)]
    if n == 2:
        return [(values[0] + values[1], None), (values[0] - values[1], None)]
    even = real_transform(values[0::2])
    odd = real_transform(values[1::2])
    out = [None] * (n // 2 + 1)
    h = n // 2
    for k in range(n // 4 + 1):
        er, ei = even[k]
        o_r, o_i = odd[k]
        if k == 0:
            out[0] = (er + o_r, None)
            out[h] = (er - o_r, None)
        elif k == n // 4:
            out[k] = (er, -o_r)
        else:
            tr, ti = times_root(o_r, o_i, k, n, -1)
            out[k] = (er + tr, ei + ti)
            out[h - k] = (er - tr, ti - ei)
    return out


def minmod(p, q):
    return jnp.minimum(jnp.maximum(p, jnp.minimum(q, 0.0)), jnp.maximum(q, 0.0))


def turned(v, by):
    n = v.shape[-2]
    if by > 0:
        return jnp.concatenate([v[..., n - 1 :, :], v[..., : n - 1, :]], axis=-2)
    return jnp.concatenate([v[..., 1:, :], v[..., :1, :]], axis=-2)


def moved(g, low, high, positive, vel_x, vel_y, vel_z, zs):
    sign = 0.5 if positive else -0.5
    here = g[zs[0] : zs[-1] + 1]
    planes = jnp.concatenate([low, here, high], axis=1)
    d = planes[:, 1:] - planes[:, :-1]
    face = planes[:, 1:4] + sign * minmod(d[:, :-1], d[:, 1:])
    jump_x = face[:, 1:] - face[:, :-1]

    up_y = vel_y > 0.0
    half_y = jnp.where(up_y, 0.5, -0.5)
    d = here - turned(here, 1)
    face = here + half_y * minmod(d, turned(d, -1))
    e = face - turned(face, 1)
    jump_y = jnp.where(up_y, e, turned(e, -1))

    up_z = vel_z > 0.0
    half_z = jnp.where(up_z, 0.5, -0.5)
    d = [g[z] - g[(z + 3) % 4] for z in range(4)]
    face = [g[z] + half_z * minmod(d[z], d[(z + 1) % 4]) for z in range(4)]
    e = [face[z] - face[(z + 3) % 4] for z in range(4)]
    jump_z = jnp.stack([jnp.where(up_z, e[z], e[(z + 1) % 4]) for z in zs])
    return here - courant * (vel_x * jump_x + vel_y * jump_y + vel_z * jump_z)


def lane_velocities(c_hi):
    lane = lax.broadcasted_iota(jnp.int32, (1, 128), 1)
    vel_x = (2.0 * ((lane >> 4) + 8 * c_hi).astype(f32) + 1.0) / M - 1.0
    vel_y = (2.0 * (lane & 15).astype(f32) + 1.0) / M - 1.0
    return vel_x, vel_y


def level(a):
    return (2.0 * a.astype(f32) + 1.0) / M - 1.0


def split(v):
    hi = v.astype(bf16)
    lo = (v - hi.astype(f32)).astype(bf16)
    return hi, lo


def product(v, weights):
    hi, lo = split(v)
    return jnp.dot(
        jnp.concatenate([hi, lo, hi], axis=1), weights, preferred_element_type=f32
    )


def parted(v):
    return jnp.concatenate([v[:, 16 * c : 16 * c + 16] for c in (*range(0, M, 2), *range(1, M, 2))], axis=1)


def relaxed_cells(k, x_ref, tables, w_forward, w_inverse, spec, gain, out_ref):
    rows = [
        jnp.concatenate([x_ref[k, a, 0] + x_ref[k, a, 1], x_ref[k, a, 0] - x_ref[k, a, 1]], axis=1)
        * (1.0 / M**3)
        for a in range(M)
    ]
    modes = real_transform(rows)
    parts = [re for re, _ in modes] + [im for _, im in modes[1:8]]
    parts = jnp.concatenate(parts, axis=0)
    both = [product(parts[:, 128 * r : 128 * r + 128], w_forward[r]) for r in range(2)]
    cosines, sines = (
        jnp.concatenate([part[:, 128 * i : 128 * i + 128] for part in both], axis=1) for i in range(2)
    )
    cosines = [cosines[8 * i : 8 * i + 8] for i in range(16)]
    sines = [sines[8 * i : 8 * i + 8] for i in range(16)]
    for q in range(9):
        rc, rs = cosines[q], sines[q]
        if q in (0, 8):
            spec[q, 0] = rc
            spec[q, 1] = -rs
            continue
        ic, js = cosines[q + 8], sines[q + 8]
        spec[q, 0] = rc + js
        spec[q, 1] = ic - rs
        spec[16 - q, 0] = rc - js
        spec[16 - q, 1] = -ic - rs

    def bent(m):
        values = []
        for q in range(M):
            t = tables[m, q]
            values.append((t * spec[q, 0], t * spec[q, 1]))
        values = transform(values, 1)
        return [
            jnp.concatenate(
                [
                    jnp.concatenate([v[:, 128 * r : 128 * r + 128] for v in pair], axis=1)
                    for pair in values
                ],
                axis=0,
            )
            for r in range(2)
        ]

    loss = [product(half, w_inverse[r, :, :128]) for r, half in enumerate(bent(8))]
    for c in range(2):
        held = jnp.concatenate([x_ref[k, a, c] for a in range(M)], axis=0)
        total_loss = loss[0] + loss[1] if c == 0 else loss[0] - loss[1]
        gain[:, 128 * c : 128 * c + 128] = -(held * total_loss)

    for p in range(4):
        halves = [
            product(jnp.concatenate([left, right], axis=0), w_inverse[r])
            for r, (left, right) in enumerate(zip(bent(p), bent(p + 4)))
        ]
        for c in range(2):
            both = halves[0] + halves[1] if c == 0 else halves[0] - halves[1]
            left, right = both[:128], both[128:]
            gain[:, 128 * c : 128 * c + 128] += (
                left[:, :128] * right[:, :128] - left[:, 128:] * right[:, 128:]
            )

    velocities = [lane_velocities(c) for c in range(2)]
    weight = (2.0 / M) ** 3
    vz = [(2.0 * a + 1.0) / M - 1.0 for a in range(M)]
    cells = [x_ref[k, a] for a in range(M)]
    s0 = sum(cells[1:], cells[0])
    s1 = sum((cells[a] * vz[a] for a in range(1, M)), cells[0] * vz[0])
    s2 = sum((cells[a] * (vz[a] * vz[a]) for a in range(1, M)), cells[0] * (vz[0] * vz[0]))

    def total(v):
        return jnp.sum(v, axis=-1, keepdims=True) * weight

    (vx0, vy0), (vx1, vy1) = velocities
    mass = total(s0[0] + s0[1])
    mean_x = total(s0[0] * vx0 + s0[1] * vx1) / mass
    mean_y = total(s0[0] * vy0 + s0[1] * vy1) / mass
    mean_z = total(s1[0] + s1[1]) / mass
    energy = (
        total(
            s0[0] * (vx0 * vx0 + vy0 * vy0) + s0[1] * (vx1 * vx1 + vy1 * vy1) + s2[0] + s2[1]
        )
        / mass
    )
    heat = (energy - (mean_x * mean_x + mean_y * mean_y + mean_z * mean_z)) / 3.0
    variance = 2.0 * math.pi * heat
    rate = rate_scale * mass
    scale = time_step * rate * mass / (variance * jnp.sqrt(variance))
    inverse_heat = -1.0 / (2.0 * heat)
    divisor = 1.0 / (1.0 + time_step * rate)
    flat = [(vx - mean_x) ** 2 + (vy - mean_y) ** 2 for vx, vy in velocities]
    for a in range(M):
        away = (vz[a] - mean_z) ** 2
        for c in range(2):
            maxwell = scale * jnp.exp((flat[c] + away) * inverse_heat)
            change = gain[8 * a : 8 * a + 8, 128 * c : 128 * c + 128]
            out_ref[k, a, c] = (x_ref[k, a, c] + time_step * change + maxwell) * divisor


def kernel(
    density,
    gl_far,
    gr_far,
    lk_far,
    w_forward_far,
    w_inverse_far,
    out,
    raw,
    gl,
    gr,
    lk,
    w_forward,
    w_inverse,
    g,
    halo_a,
    halo_b,
    adv,
    cells,
    ready,
    field,
    tables,
    spec,
    gain,
    halo_send,
    halo_recv,
    out_send,
    out_recv,
    back_send,
    back_recv,
    local_sem,
    load_sem,
    far_send,
    far_recv,
    ack,
):
    s = lax.axis_index("space")
    j = lax.axis_index("vel")
    count = lax.axis_size("space")
    after = (lax.rem(s + 1, count), j)
    before = (lax.rem(s + count - 1, count), j)
    order = [sorted((d for d in range(NP) if d != i), key=lambda d: -abs(d - i)) for i in range(NP)]
    peers = []
    for n in range(NP - 1):
        d = jnp.int32(order[0][n])
        for i in range(1, NP):
            d = jnp.where(j == i, order[i][n], d)
        peers.append(d)

    place_in_run = lax.rem(s, RUN)
    is_first, is_last = place_in_run == 0, place_in_run == RUN - 1
    is_edge = jnp.logical_or(is_first, is_last)
    is_inner = jnp.logical_not(is_edge)
    far_s = jnp.where(is_first, before[0], after[0])

    barrier = pltpu.get_barrier_semaphore()

    def tell(d):
        pl.semaphore_signal(barrier, inc=1, device_id=d, device_id_type=MESH)

    @pl.when(is_edge)
    def _():
        tell((far_s, j))

    @pl.when(jnp.logical_and(is_inner, place_in_run != RUN - 2))
    def _():
        tell(after)

    @pl.when(jnp.logical_and(is_inner, place_in_run != 1))
    def _():
        tell(before)

    @pl.when(is_first)
    def _():
        tell(after)

    @pl.when(is_last)
    def _():
        tell(before)

    for d in peers:
        tell((s, d))

    loads = [
        pltpu.make_async_copy(density, raw, load_sem.at[0]),
        pltpu.make_async_copy(w_forward_far, w_forward, load_sem.at[1]),
        pltpu.make_async_copy(w_inverse_far, w_inverse, load_sem.at[2]),
        pltpu.make_async_copy(gl_far, gl, load_sem.at[3]),
        pltpu.make_async_copy(gr_far, gr, load_sem.at[4]),
        pltpu.make_async_copy(lk_far, lk, load_sem.at[5]),
    ]
    for load in loads:
        load.start()
    loads[0].wait()
    for x in range(2):
        for z in range(4):
            for t in range(4):
                g[z, t // 2, t % 2, x] = raw[x, :, z, 128 * t : 128 * t + 128]
    def halo_copies(step, source, landing, k):
        low, high = landing
        zs = pl.ds(2 * k, 2)
        pairs = (
            (source.at[zs, :, 1], low.at[zs, :, 1], after),
            (source.at[zs, :, 0, 1], low.at[zs, :, 0, 1], after),
            (source.at[zs, :, 0], high.at[zs, :, 0], before),
            (source.at[zs, :, 1, 0], high.at[zs, :, 1, 0], before),
        )
        return [
            pltpu.make_async_remote_copy(
                src_ref=src,
                dst_ref=dst,
                send_sem=halo_send.at[step, k, i],
                recv_sem=halo_recv.at[step, k, i],
                device_id=d,
                device_id_type=MESH,
            )
            for i, (src, dst, d) in enumerate(pairs)
        ]

    def planes_beside(landing, a_l, c_hi, zs):
        low, high = landing
        if c_hi:
            return low[zs, a_l, 1], high[zs, a_l, 1, 0:1]
        return low[zs, a_l, 0, 1:2], high[zs, a_l, 0]

    def out_copy(k, d):
        return pltpu.make_async_remote_copy(
            src_ref=adv.at[k, d],
            dst_ref=cells.at[k, pl.ds(2 * j, 2)],
            send_sem=out_send.at[k, d],
            recv_sem=out_recv.at[k, j],
            device_id=(s, d),
            device_id_type=MESH,
        )

    def arrival(k, d, dst, sem):
        return pltpu.make_async_remote_copy(
            src_ref=adv.at[k, d],
            dst_ref=dst,
            send_sem=out_send.at[k, d],
            recv_sem=sem.at[k, d],
            device_id=(s, d),
            device_id_type=MESH,
        )

    def place(k, owner):
        return field.at[
            2 * k + lax.rem(lax.div(owner, 2), 2),
            :,
            :,
            lax.div(owner, 4),
            pl.ds(pl.multiple_of(8 * lax.rem(owner, 2), 8), 8),
        ]

    def back_copy(k, d):
        return pltpu.make_async_remote_copy(
            src_ref=ready.at[k, pl.ds(2 * d, 2)],
            dst_ref=place(k, j),
            send_sem=back_send.at[k, d],
            recv_sem=back_recv.at[k, j],
            device_id=(s, d),
            device_id_type=MESH,
        )

    def far_copy(k, owner, d, sem, side, both):
        low, high = halo_b
        x = lax.div(owner, 4) if not isinstance(owner, int) else owner // 4
        z = 2 * k + (lax.rem(lax.div(owner, 2), 2) if not isinstance(owner, int) else owner // 2 % 2)
        odd = lax.rem(owner, 2) if not isinstance(owner, int) else owner % 2
        ys = pl.ds(8 * odd if isinstance(owner, int) else pl.multiple_of(8 * odd, 8), 8)
        there = low if side else high
        if both:
            src, dst = ready.at[k, pl.ds(2 * d, 2)], there.at[z, :, :, x, ys]
        else:
            src, dst = ready.at[k, pl.ds(2 * d, 2), side], there.at[z, :, side, x, ys]
        return pltpu.make_async_remote_copy(
            src_ref=src,
            dst_ref=dst,
            send_sem=far_send.at[k, d],
            recv_sem=far_recv.at[k, sem],
            device_id=(far_s, d),
            device_id_type=MESH,
        )

    def each_far(act, k):
        for side, here in ((1, is_last), (0, is_first)):
            for x in range(2):

                @pl.when(jnp.logical_and(here, lax.div(j, 4) == x))
                def _():
                    for d in (j, *reversed(peers)):
                        act(far_copy(k, j, d, j, side, x == side))

    def await_far(k):
        for side, here in ((1, is_first), (0, is_last)):

            @pl.when(here)
            def _():
                for owner in range(NP):
                    far_copy(k, owner, 0, owner, side, owner // 4 == side).wait_recv()

    first = [halo_copies(0, g, halo_a, k) for k in range(CH)]

    def start(copies):
        for copy in copies:
            copy.start()

    @pl.when(is_inner)
    def _():
        pl.semaphore_wait(barrier, NP + 1)

    @pl.when(place_in_run == 1)
    def _():
        pl.semaphore_signal(ack, inc=1, device_id=before, device_id_type=MESH)

    @pl.when(place_in_run == RUN - 2)
    def _():
        pl.semaphore_signal(ack, inc=1, device_id=after, device_id_type=MESH)

    @pl.when(is_edge)
    def _():
        pl.semaphore_wait(ack, 1)

    def start_near(copies):
        pl.when(jnp.logical_not(is_last))(lambda: start(copies[:2]))
        pl.when(jnp.logical_not(is_first))(lambda: start(copies[2:]))

    for k in range(CH):
        start_near(first[k])

    @pl.when(is_edge)
    def _():
        pl.semaphore_wait(barrier, NP)

    def start_far(copies):
        pl.when(is_last)(lambda: start(copies[:2]))
        pl.when(is_first)(lambda: start(copies[2:]))

    start_far(first[0])
    for load in loads[1:]:
        load.wait()
    for q in range(M):
        modes = slice(256 * q, 256 * q + 256)
        lefts, rights, lost = parted(gl[:, modes]), parted(gr[:, modes]), parted(lk[:, modes])
        for p in range(4):
            tables[p, q] = jnp.broadcast_to(lefts[p : p + 1], (8, 256))
            tables[p + 4, q] = jnp.broadcast_to(rights[p : p + 1], (8, 256))
        tables[8, q] = jnp.broadcast_to(lost, (8, 256))
    start_far(first[1])

    outs = [[out_copy(k, d) for d in peers] for k in range(CH)]
    own_out = [
        pltpu.make_async_copy(adv.at[k, j], cells.at[k, pl.ds(2 * j, 2)], local_sem.at[0, k])
        for k in range(CH)
    ]
    for k in range(CH):
        for copy in first[k]:
            copy.wait_recv()

        def advance(a_l, c):
            vel_z = jnp.full((1, 128), level(2 * j + a_l), f32)
            for c_hi in range(2):
                vel_x, vel_y = lane_velocities(c_hi)
                low, high = planes_beside(halo_a, a_l, c_hi, pl.ds(2 * k, 2))
                new = moved(
                    g[:, a_l, c_hi], low, high, c_hi == 1, vel_x, vel_y, vel_z, (2 * k, 2 * k + 1)
                )
                for x in range(2):
                    for z in range(2):
                        for h in range(2):
                            adv[k, 4 * x + 2 * z + h, a_l, c_hi] = new[z, x, 8 * h : 8 * h + 8]
            return c

        lax.fori_loop(0, 2, advance, 0)
        for copy in outs[k]:
            copy.start()
        own_out[k].start()

    backs = [[back_copy(k, d) for d in peers] for k in range(CH)]
    own_back = [
        pltpu.make_async_copy(ready.at[k, pl.ds(2 * j, 2)], place(k, j), local_sem.at[1, k])
        for k in range(CH)
    ]
    for k in range(CH):
        own_out[k].wait()
        for d in peers:
            arrival(k, d, cells.at[k, pl.ds(2 * d, 2)], out_recv).wait_recv()
        relaxed_cells(k, cells, tables, w_forward, w_inverse, spec, gain, ready)
        each_far(lambda copy: copy.start(), k)
        for copy in backs[k]:
            copy.start()
        own_back[k].start()

    second = [halo_copies(1, field, halo_b, k) for k in range(CH)]
    for k in range(CH):
        own_back[k].wait()
        for d in peers:
            arrival(k, d, place(k, d), back_recv).wait_recv()
        start_near(second[k])
    for k in range(CH):
        pl.when(jnp.logical_not(is_first))(lambda k=k: [copy.wait_recv() for copy in second[k][:2]] and None)
        pl.when(jnp.logical_not(is_last))(lambda k=k: [copy.wait_recv() for copy in second[k][2:]] and None)
        await_far(k)

    def finish(a_l):
        vel_z = jnp.full((1, 128), level(2 * j + a_l), f32)
        for c_hi in range(2):
            vel_x, vel_y = lane_velocities(c_hi)
            low, high = planes_beside(halo_b, a_l, c_hi, pl.ds(0, 4))
            new = moved(
                field[:, a_l, c_hi], low, high, c_hi == 1, vel_x, vel_y, vel_z, (0, 1, 2, 3)
            )
            lanes = slice(128 * (2 * a_l + c_hi), 128 * (2 * a_l + c_hi + 1))
            for x in range(2):
                for z in range(4):
                    out[x, :, z, lanes] = new[z, x]

    finish(0)
    finish(1)
    for group in (*first, *outs, *backs):
        for copy in group:
            copy.wait_send()
    for k in range(CH):
        pl.when(jnp.logical_not(is_last))(lambda k=k: [copy.wait_send() for copy in second[k][:2]] and None)
        pl.when(jnp.logical_not(is_first))(lambda k=k: [copy.wait_send() for copy in second[k][2:]] and None)
        each_far(lambda copy: copy.wait_send(), k)


def weights():
    index = np.arange(128)
    forward, inverse = [], []

    def held(m):
        m = m.astype(np.float32)
        hi = m.astype(jnp.bfloat16)
        lo = (m - hi.astype(np.float32)).astype(jnp.bfloat16)
        return np.concatenate([hi, hi, lo], axis=0)

    for r in range(2):
        mode, speed = index[:, None], index[None, :]
        phase = ((2 * (mode // 16) + r) * (speed // 16) + (mode % 16) * (speed % 16)) % 16
        cos, sin = np.cos(phase * (np.pi / 8)), np.sin(phase * (np.pi / 8))
        forward.append(held(np.concatenate([cos.T, sin.T], axis=1)))
        inverse.append(held(np.block([[cos, sin], [-sin, cos]])))
    return np.stack(forward), np.stack(inverse)


def per_device(density, gain_left, gain_right, loss_kernel):
    forward, inverse = weights()
    held = (4, 2, 2, 2, 16, 128)
    far = pl.BlockSpec(memory_space=pltpu.HBM)
    vmem = pl.BlockSpec(memory_space=pltpu.VMEM)
    dma = pltpu.SemaphoreType.DMA
    landing = (pltpu.VMEM(held, f32), pltpu.VMEM(held, f32))
    return pl.pallas_call(
        kernel,
        out_shape=jax.ShapeDtypeStruct(density.shape, f32),
        in_specs=[far] * 6,
        out_specs=vmem,
        scratch_shapes=[
            pltpu.VMEM(density.shape, f32),
            pltpu.VMEM(gain_left.shape, f32),
            pltpu.VMEM(gain_right.shape, f32),
            pltpu.VMEM((1, loss_kernel.shape[0]), f32),
            pltpu.VMEM(forward.shape, bf16),
            pltpu.VMEM(inverse.shape, bf16),
            pltpu.VMEM(held, f32),
            landing,
            landing,
            pltpu.VMEM((CH, NP, 2, 2, 8, 128), f32),
            pltpu.VMEM((CH, M, 2, 8, 128), f32),
            pltpu.VMEM((CH, M, 2, 8, 128), f32),
            pltpu.VMEM(held, f32),
            pltpu.VMEM((9, M, 8, 256), f32),
            pltpu.VMEM((M, 2, 8, 256), f32),
            pltpu.VMEM((128, 256), f32),
            dma((2, CH, 4)),
            dma((2, CH, 4)),
            dma((CH, NP)),
            dma((CH, NP)),
            dma((CH, NP)),
            dma((CH, NP)),
            dma((2, CH)),
            dma((6,)),
            dma((CH, NP)),
            dma((CH, NP)),
            pltpu.SemaphoreType.REGULAR,
        ],
        compiler_params=pltpu.CompilerParams(
            collective_id=0, has_side_effects=True, vmem_limit_bytes=63 * 1024 * 1024
        ),
    )(density, gain_left, gain_right, loss_kernel.reshape(1, -1), jnp.asarray(forward), jnp.asarray(inverse))


def solution(mesh):
    in_specs = (P("space", None, None, "vel"), P(), P(), P())
    out_specs = P("space", None, None, "vel")
    return jax.shard_map(
        per_device, mesh=mesh, in_specs=in_specs, out_specs=out_specs, check_vma=False
    )
```

```python
import math

import jax
import jax.numpy as jnp
import numpy as np
from jax import lax
from jax.experimental import pallas as pl
from jax.experimental.pallas import tpu as pltpu
from jax.sharding import PartitionSpec as P

MESH = pl.DeviceIdType.MESH
M = 16
NP = 8
RUN = 8
CH = 2
courant = 1.0 / 6.0
time_step = 0.25
rate_scale = 0.25
f32 = jnp.float32
bf16 = jnp.bfloat16


def times_root(re, im, k, n, sign):
    k = k % n
    if k == 0:
        return re, im
    if 4 * k == n:
        return (-im, re) if sign > 0 else (im, -re)
    if 2 * k == n:
        return -re, -im
    if 4 * k == 3 * n:
        return (im, -re) if sign > 0 else (-im, re)
    c, s = math.cos(2 * math.pi * k / n), sign * math.sin(2 * math.pi * k / n)
    if 8 * k % n == 0:
        r = math.sqrt(0.5)
        cs, ss = (1 if c > 0 else -1), (1 if s > 0 else -1)
        a = re if cs > 0 else -re
        b = im if ss > 0 else -im
        d = re if ss > 0 else -re
        e = im if cs > 0 else -im
        return (a - b) * r, (d + e) * r
    return re * c - im * s, re * s + im * c


def transform(values, sign):
    n = len(values)
    if n == 1:
        return values
    even = transform(values[0::2], sign)
    odd = transform(values[1::2], sign)
    out = [None] * n
    for k in range(n // 2):
        tr, ti = times_root(*odd[k], k, n, sign)
        er, ei = even[k]
        out[k] = (er + tr, ei + ti)
        out[k + n // 2] = (er - tr, ei - ti)
    return out


def real_transform(values):
    n = len(values)
    if n == 1:
        return [(values[0], None)]
    if n == 2:
        return [(values[0] + values[1], None), (values[0] - values[1], None)]
    even = real_transform(values[0::2])
    odd = real_transform(values[1::2])
    out = [None] * (n // 2 + 1)
    h = n // 2
    for k in range(n // 4 + 1):
        er, ei = even[k]
        o_r, o_i = odd[k]
        if k == 0:
            out[0] = (er + o_r, None)
            out[h] = (er - o_r, None)
        elif k == n // 4:
            out[k] = (er, -o_r)
        else:
            tr, ti = times_root(o_r, o_i, k, n, -1)
            out[k] = (er + tr, ei + ti)
            out[h - k] = (er - tr, ti - ei)
    return out


def minmod(p, q):
    return jnp.minimum(jnp.maximum(p, jnp.minimum(q, 0.0)), jnp.maximum(q, 0.0))


def turned(v, by):
    n = v.shape[-2]
    if by > 0:
        return jnp.concatenate([v[..., n - 1 :, :], v[..., : n - 1, :]], axis=-2)
    return jnp.concatenate([v[..., 1:, :], v[..., :1, :]], axis=-2)


def moved(g, low, high, positive, vel_x, vel_y, vel_z, zs):
    sign = 0.5 if positive else -0.5
    here = g[zs[0] : zs[-1] + 1]
    planes = jnp.concatenate([low, here, high], axis=1)
    d = planes[:, 1:] - planes[:, :-1]
    face = planes[:, 1:4] + sign * minmod(d[:, :-1], d[:, 1:])
    jump_x = face[:, 1:] - face[:, :-1]

    up_y = vel_y > 0.0
    half_y = jnp.where(up_y, 0.5, -0.5)
    d = here - turned(here, 1)
    face = here + half_y * minmod(d, turned(d, -1))
    e = face - turned(face, 1)
    jump_y = jnp.where(up_y, e, turned(e, -1))

    up_z = vel_z > 0.0
    half_z = jnp.where(up_z, 0.5, -0.5)
    d = [g[z] - g[(z + 3) % 4] for z in range(4)]
    face = [g[z] + half_z * minmod(d[z], d[(z + 1) % 4]) for z in range(4)]
    e = [face[z] - face[(z + 3) % 4] for z in range(4)]
    jump_z = jnp.stack([jnp.where(up_z, e[z], e[(z + 1) % 4]) for z in zs])
    return here - courant * (vel_x * jump_x + vel_y * jump_y + vel_z * jump_z)


def lane_velocities(c_hi):
    lane = lax.broadcasted_iota(jnp.int32, (1, 128), 1)
    vel_x = (2.0 * ((lane >> 4) + 8 * c_hi).astype(f32) + 1.0) / M - 1.0
    vel_y = (2.0 * (lane & 15).astype(f32) + 1.0) / M - 1.0
    return vel_x, vel_y


def level(a):
    return (2.0 * a.astype(f32) + 1.0) / M - 1.0


def split(v):
    hi = v.astype(bf16)
    lo = (v - hi.astype(f32)).astype(bf16)
    return hi, lo


def product(v, weights):
    hi, lo = split(v)
    return jnp.dot(
        jnp.concatenate([hi, lo, hi], axis=1), weights, preferred_element_type=f32
    )


def parted(v):
    return jnp.concatenate([v[:, 16 * c : 16 * c + 16] for c in (*range(0, M, 2), *range(1, M, 2))], axis=1)


def relaxed_cells(k, x_ref, tables, w_forward, w_inverse, spec, gain, out_ref):
    rows = [
        jnp.concatenate([x_ref[k, a, 0] + x_ref[k, a, 1], x_ref[k, a, 0] - x_ref[k, a, 1]], axis=1)
        * (1.0 / M**3)
        for a in range(M)
    ]
    modes = real_transform(rows)
    parts = [re for re, _ in modes] + [im for _, im in modes[1:8]]
    parts = jnp.concatenate(parts, axis=0)
    both = [product(parts[:, 128 * r : 128 * r + 128], w_forward[r]) for r in range(2)]
    cosines, sines = (
        jnp.concatenate([part[:, 128 * i : 128 * i + 128] for part in both], axis=1) for i in range(2)
    )
    cosines = [cosines[8 * i : 8 * i + 8] for i in range(16)]
    sines = [sines[8 * i : 8 * i + 8] for i in range(16)]
    for q in range(9):
        rc, rs = cosines[q], sines[q]
        if q in (0, 8):
            spec[q, 0] = rc
            spec[q, 1] = -rs
            continue
        ic, js = cosines[q + 8], sines[q + 8]
        spec[q, 0] = rc + js
        spec[q, 1] = ic - rs
        spec[16 - q, 0] = rc - js
        spec[16 - q, 1] = -ic - rs

    def bent(m):
        values = []
        for q in range(M):
            t = tables[m, q]
            values.append((t * spec[q, 0], t * spec[q, 1]))
        values = transform(values, 1)
        return [
            jnp.concatenate(
                [
                    jnp.concatenate([v[:, 128 * r : 128 * r + 128] for v in pair], axis=1)
                    for pair in values
                ],
                axis=0,
            )
            for r in range(2)
        ]

    loss = [product(half, w_inverse[r, :, :128]) for r, half in enumerate(bent(8))]
    for c in range(2):
        held = jnp.concatenate([x_ref[k, a, c] for a in range(M)], axis=0)
        total_loss = loss[0] + loss[1] if c == 0 else loss[0] - loss[1]
        gain[:, 128 * c : 128 * c + 128] = -(held * total_loss)

    for p in range(4):
        halves = [
            product(jnp.concatenate([left, right], axis=0), w_inverse[r])
            for r, (left, right) in enumerate(zip(bent(p), bent(p + 4)))
        ]
        for c in range(2):
            both = halves[0] + halves[1] if c == 0 else halves[0] - halves[1]
            left, right = both[:128], both[128:]
            gain[:, 128 * c : 128 * c + 128] += (
                left[:, :128] * right[:, :128] - left[:, 128:] * right[:, 128:]
            )

    velocities = [lane_velocities(c) for c in range(2)]
    weight = (2.0 / M) ** 3
    vz = [(2.0 * a + 1.0) / M - 1.0 for a in range(M)]
    cells = [x_ref[k, a] for a in range(M)]
    s0 = sum(cells[1:], cells[0])
    s1 = sum((cells[a] * vz[a] for a in range(1, M)), cells[0] * vz[0])
    s2 = sum((cells[a] * (vz[a] * vz[a]) for a in range(1, M)), cells[0] * (vz[0] * vz[0]))

    def total(v):
        return jnp.sum(v, axis=-1, keepdims=True) * weight

    (vx0, vy0), (vx1, vy1) = velocities
    mass = total(s0[0] + s0[1])
    mean_x = total(s0[0] * vx0 + s0[1] * vx1) / mass
    mean_y = total(s0[0] * vy0 + s0[1] * vy1) / mass
    mean_z = total(s1[0] + s1[1]) / mass
    energy = (
        total(
            s0[0] * (vx0 * vx0 + vy0 * vy0) + s0[1] * (vx1 * vx1 + vy1 * vy1) + s2[0] + s2[1]
        )
        / mass
    )
    heat = (energy - (mean_x * mean_x + mean_y * mean_y + mean_z * mean_z)) / 3.0
    variance = 2.0 * math.pi * heat
    rate = rate_scale * mass
    scale = time_step * rate * mass / (variance * jnp.sqrt(variance))
    inverse_heat = -1.0 / (2.0 * heat)
    divisor = 1.0 / (1.0 + time_step * rate)
    flat = [(vx - mean_x) ** 2 + (vy - mean_y) ** 2 for vx, vy in velocities]
    for a in range(M):
        away = (vz[a] - mean_z) ** 2
        for c in range(2):
            maxwell = scale * jnp.exp((flat[c] + away) * inverse_heat)
            change = gain[8 * a : 8 * a + 8, 128 * c : 128 * c + 128]
            out_ref[k, a, c] = (x_ref[k, a, c] + time_step * change + maxwell) * divisor


def kernel(
    density,
    gl_far,
    gr_far,
    lk_far,
    w_forward_far,
    w_inverse_far,
    out,
    raw,
    gl,
    gr,
    lk,
    w_forward,
    w_inverse,
    g,
    halo_a,
    halo_b,
    adv,
    cells,
    ready,
    field,
    tables,
    spec,
    gain,
    halo_send,
    halo_recv,
    out_send,
    out_recv,
    back_send,
    back_recv,
    local_sem,
    load_sem,
    far_send,
    far_recv,
    ack,
    passing_two,
    passing_one,
    pass_send,
    pass_recv,
    go,
):
    s = lax.axis_index("space")
    j = lax.axis_index("vel")
    count = lax.axis_size("space")
    after = (lax.rem(s + 1, count), j)
    before = (lax.rem(s + count - 1, count), j)
    order = [sorted((d for d in range(NP) if d != i), key=lambda d: -abs(d - i)) for i in range(NP)]
    peers = []
    for n in range(NP - 1):
        d = jnp.int32(order[0][n])
        for i in range(1, NP):
            d = jnp.where(j == i, order[i][n], d)
        peers.append(d)

    place_in_run = lax.rem(s, RUN)
    is_first, is_last = place_in_run == 0, place_in_run == RUN - 1
    is_edge = jnp.logical_or(is_first, is_last)
    is_inner = jnp.logical_not(is_edge)
    far_s = jnp.where(is_first, before[0], after[0])

    barrier = pltpu.get_barrier_semaphore()

    def tell(d):
        pl.semaphore_signal(barrier, inc=1, device_id=d, device_id_type=MESH)

    @pl.when(is_edge)
    def _():
        tell((far_s, j))

    @pl.when(jnp.logical_and(is_inner, place_in_run != RUN - 2))
    def _():
        tell(after)

    @pl.when(jnp.logical_and(is_inner, place_in_run != 1))
    def _():
        tell(before)

    @pl.when(is_first)
    def _():
        tell(after)

    @pl.when(is_last)
    def _():
        tell(before)

    for d in peers:
        tell((s, d))

    loads = [
        pltpu.make_async_copy(density, raw, load_sem.at[0]),
        pltpu.make_async_copy(w_forward_far, w_forward, load_sem.at[1]),
        pltpu.make_async_copy(w_inverse_far, w_inverse, load_sem.at[2]),
        pltpu.make_async_copy(gl_far, gl, load_sem.at[3]),
        pltpu.make_async_copy(gr_far, gr, load_sem.at[4]),
        pltpu.make_async_copy(lk_far, lk, load_sem.at[5]),
    ]
    for load in loads:
        load.start()
    loads[0].wait()
    for x in range(2):
        for z in range(4):
            for t in range(4):
                g[z, t // 2, t % 2, x] = raw[x, :, z, 128 * t : 128 * t + 128]
    def halo_copies(step, source, landing, k):
        low, high = landing
        zs = pl.ds(2 * k, 2)
        pairs = (
            (source.at[zs, :, 1], low.at[zs, :, 1], after),
            (source.at[zs, :, 0, 1], low.at[zs, :, 0, 1], after),
            (source.at[zs, :, 0], high.at[zs, :, 0], before),
            (source.at[zs, :, 1, 0], high.at[zs, :, 1, 0], before),
        )
        return [
            pltpu.make_async_remote_copy(
                src_ref=src,
                dst_ref=dst,
                send_sem=halo_send.at[step, k, i],
                recv_sem=halo_recv.at[step, k, i],
                device_id=d,
                device_id_type=MESH,
            )
            for i, (src, dst, d) in enumerate(pairs)
        ]

    def planes_beside(landing, a_l, c_hi, zs):
        low, high = landing
        if c_hi:
            return low[zs, a_l, 1], high[zs, a_l, 1, 0:1]
        return low[zs, a_l, 0, 1:2], high[zs, a_l, 0]

    def out_copy(k, d):
        return pltpu.make_async_remote_copy(
            src_ref=adv.at[k, d],
            dst_ref=cells.at[k, pl.ds(2 * j, 2)],
            send_sem=out_send.at[k, d],
            recv_sem=out_recv.at[k, j],
            device_id=(s, d),
            device_id_type=MESH,
        )

    def arrival(k, d, dst, sem):
        return pltpu.make_async_remote_copy(
            src_ref=adv.at[k, d],
            dst_ref=dst,
            send_sem=out_send.at[k, d],
            recv_sem=sem.at[k, d],
            device_id=(s, d),
            device_id_type=MESH,
        )

    def place(k, owner):
        return field.at[
            2 * k + lax.rem(lax.div(owner, 2), 2),
            :,
            :,
            lax.div(owner, 4),
            pl.ds(pl.multiple_of(8 * lax.rem(owner, 2), 8), 8),
        ]

    def back_copy(k, d):
        return pltpu.make_async_remote_copy(
            src_ref=ready.at[k, pl.ds(2 * d, 2)],
            dst_ref=place(k, j),
            send_sem=back_send.at[k, d],
            recv_sem=back_recv.at[k, j],
            device_id=(s, d),
            device_id_type=MESH,
        )

    def far_copy(k, owner, d, sem, side, both):
        low, high = halo_b
        x = lax.div(owner, 4) if not isinstance(owner, int) else owner // 4
        z = 2 * k + (lax.rem(lax.div(owner, 2), 2) if not isinstance(owner, int) else owner // 2 % 2)
        odd = lax.rem(owner, 2) if not isinstance(owner, int) else owner % 2
        ys = pl.ds(8 * odd if isinstance(owner, int) else pl.multiple_of(8 * odd, 8), 8)
        there = low if side else high
        if both:
            src, dst = ready.at[k, pl.ds(2 * d, 2)], there.at[z, :, :, x, ys]
        else:
            src, dst = ready.at[k, pl.ds(2 * d, 2), side], there.at[z, :, side, x, ys]
        return pltpu.make_async_remote_copy(
            src_ref=src,
            dst_ref=dst,
            send_sem=far_send.at[k, d],
            recv_sem=far_recv.at[k, sem],
            device_id=(far_s, d),
            device_id_type=MESH,
        )

    def each_far(act, k):
        for side, here in ((1, is_last), (0, is_first)):
            for x in range(2):

                @pl.when(jnp.logical_and(here, lax.div(j, 4) == x))
                def _():
                    for d in (j, *reversed(peers)):
                        act(far_copy(k, j, d, j, side, x == side))

    def await_far(k):
        for side, here in ((1, is_first), (0, is_last)):

            @pl.when(here)
            def _():
                for owner in range(NP):
                    far_copy(k, owner, 0, owner, side, owner // 4 == side).wait_recv()

    first = [halo_copies(0, g, halo_a, k) for k in range(CH)]

    def start(copies):
        for copy in copies:
            copy.start()

    @pl.when(is_inner)
    def _():
        pl.semaphore_wait(barrier, NP + 1)

    @pl.when(place_in_run == 1)
    def _():
        pl.semaphore_signal(ack, inc=1, device_id=before, device_id_type=MESH)

    @pl.when(place_in_run == RUN - 2)
    def _():
        pl.semaphore_signal(ack, inc=1, device_id=after, device_id_type=MESH)

    @pl.when(is_edge)
    def _():
        pl.semaphore_wait(ack, 1)

    def start_near(copies):
        pl.when(jnp.logical_not(is_last))(lambda: start(copies[:2]))
        pl.when(jnp.logical_not(is_first))(lambda: start(copies[2:]))

    for k in range(CH):
        start_near(first[k])

    def handed(step):
        zs = pl.ds(2, 2)
        if step == 0:
            ends = (
                (g.at[zs, :, 1], passing_two, g.at[zs, :, 0, 1], passing_one, is_last, s - 2),
                (g.at[zs, :, 0], passing_two, g.at[zs, :, 1, 0], passing_one, is_first, s + 2),
            )
        else:
            low, high = halo_a
            ends = (
                (
                    passing_two,
                    low.at[zs, :, 1],
                    passing_one,
                    low.at[zs, :, 0, 1],
                    place_in_run == RUN - 3,
                    lax.rem(s + 3, count),
                ),
                (
                    passing_two,
                    high.at[zs, :, 0],
                    passing_one,
                    high.at[zs, :, 1, 0],
                    place_in_run == 2,
                    lax.rem(s + count - 3, count),
                ),
            )
        found = []
        for side, (two, two_to, one, one_to, here, to) in enumerate(ends):
            copies = []
            for i, (src, dst) in enumerate(((two, two_to), (one, one_to))):
                copies.append(
                    pltpu.make_async_remote_copy(
                        src_ref=src,
                        dst_ref=dst,
                        send_sem=pass_send.at[step, i],
                        recv_sem=pass_recv.at[i] if step == 0 else halo_recv.at[0, 1, 2 * side + i],
                        device_id=(to, j),
                        device_id_type=MESH,
                    )
                )
            found.append((here, copies))
        return found

    for here, copies in handed(0):
        pl.when(here)(lambda copies=copies: start(copies))

    @pl.when(is_edge)
    def _():
        pl.semaphore_wait(barrier, NP)

    def start_far(copies):
        pl.when(is_last)(lambda: start(copies[:2]))
        pl.when(is_first)(lambda: start(copies[2:]))

    @pl.when(is_last)
    def _():
        pl.semaphore_signal(go, inc=1, device_id=(s - 2, j), device_id_type=MESH)

    @pl.when(is_first)
    def _():
        pl.semaphore_signal(go, inc=1, device_id=(s + 2, j), device_id_type=MESH)

    start_far(first[0])
    for load in loads[1:]:
        load.wait()
    for q in range(M):
        modes = slice(256 * q, 256 * q + 256)
        lefts, rights, lost = parted(gl[:, modes]), parted(gr[:, modes]), parted(lk[:, modes])
        for p in range(4):
            tables[p, q] = jnp.broadcast_to(lefts[p : p + 1], (8, 256))
            tables[p + 4, q] = jnp.broadcast_to(rights[p : p + 1], (8, 256))
        tables[8, q] = jnp.broadcast_to(lost, (8, 256))

    for here, copies in handed(1):

        @pl.when(here)
        def _(copies=copies):
            for copy in handed(0)[0][1]:
                copy.wait_recv()
            pl.semaphore_wait(go, 1)
            start(copies)
            for copy in copies:
                copy.wait_send()

    outs = [[out_copy(k, d) for d in peers] for k in range(CH)]
    own_out = [
        pltpu.make_async_copy(adv.at[k, j], cells.at[k, pl.ds(2 * j, 2)], local_sem.at[0, k])
        for k in range(CH)
    ]
    for k in range(CH):
        for copy in first[k]:
            copy.wait_recv()

        def advance(a_l, c):
            vel_z = jnp.full((1, 128), level(2 * j + a_l), f32)
            for c_hi in range(2):
                vel_x, vel_y = lane_velocities(c_hi)
                low, high = planes_beside(halo_a, a_l, c_hi, pl.ds(2 * k, 2))
                new = moved(
                    g[:, a_l, c_hi], low, high, c_hi == 1, vel_x, vel_y, vel_z, (2 * k, 2 * k + 1)
                )
                for x in range(2):
                    for z in range(2):
                        for h in range(2):
                            adv[k, 4 * x + 2 * z + h, a_l, c_hi] = new[z, x, 8 * h : 8 * h + 8]
            return c

        lax.fori_loop(0, 2, advance, 0)
        for copy in outs[k]:
            copy.start()
        own_out[k].start()

    backs = [[back_copy(k, d) for d in peers] for k in range(CH)]
    own_back = [
        pltpu.make_async_copy(ready.at[k, pl.ds(2 * j, 2)], place(k, j), local_sem.at[1, k])
        for k in range(CH)
    ]
    for k in range(CH):
        own_out[k].wait()
        for d in peers:
            arrival(k, d, cells.at[k, pl.ds(2 * d, 2)], out_recv).wait_recv()
        relaxed_cells(k, cells, tables, w_forward, w_inverse, spec, gain, ready)
        each_far(lambda copy: copy.start(), k)
        for copy in backs[k]:
            copy.start()
        own_back[k].start()

    second = [halo_copies(1, field, halo_b, k) for k in range(CH)]
    for k in range(CH):
        own_back[k].wait()
        for d in peers:
            arrival(k, d, place(k, d), back_recv).wait_recv()
        start_near(second[k])
    for k in range(CH):
        pl.when(jnp.logical_not(is_first))(lambda k=k: [copy.wait_recv() for copy in second[k][:2]] and None)
        pl.when(jnp.logical_not(is_last))(lambda k=k: [copy.wait_recv() for copy in second[k][2:]] and None)
        await_far(k)

    def finish(a_l):
        vel_z = jnp.full((1, 128), level(2 * j + a_l), f32)
        for c_hi in range(2):
            vel_x, vel_y = lane_velocities(c_hi)
            low, high = planes_beside(halo_b, a_l, c_hi, pl.ds(0, 4))
            new = moved(
                field[:, a_l, c_hi], low, high, c_hi == 1, vel_x, vel_y, vel_z, (0, 1, 2, 3)
            )
            lanes = slice(128 * (2 * a_l + c_hi), 128 * (2 * a_l + c_hi + 1))
            for x in range(2):
                for z in range(4):
                    out[x, :, z, lanes] = new[z, x]

    finish(0)
    finish(1)
    def wait_sends(copies):
        for copy in copies:
            copy.wait_send()

    for group in (first[0], *outs, *backs):
        wait_sends(group)
    pl.when(jnp.logical_not(is_last))(lambda: wait_sends(first[1][:2]))
    pl.when(jnp.logical_not(is_first))(lambda: wait_sends(first[1][2:]))
    for here, copies in handed(0):
        pl.when(here)(lambda copies=copies: wait_sends(copies))
    for k in range(CH):
        pl.when(jnp.logical_not(is_last))(lambda k=k: [copy.wait_send() for copy in second[k][:2]] and None)
        pl.when(jnp.logical_not(is_first))(lambda k=k: [copy.wait_send() for copy in second[k][2:]] and None)
        each_far(lambda copy: copy.wait_send(), k)


def weights():
    index = np.arange(128)
    forward, inverse = [], []

    def held(m):
        m = m.astype(np.float32)
        hi = m.astype(jnp.bfloat16)
        lo = (m - hi.astype(np.float32)).astype(jnp.bfloat16)
        return np.concatenate([hi, hi, lo], axis=0)

    for r in range(2):
        mode, speed = index[:, None], index[None, :]
        phase = ((2 * (mode // 16) + r) * (speed // 16) + (mode % 16) * (speed % 16)) % 16
        cos, sin = np.cos(phase * (np.pi / 8)), np.sin(phase * (np.pi / 8))
        forward.append(held(np.concatenate([cos.T, sin.T], axis=1)))
        inverse.append(held(np.block([[cos, sin], [-sin, cos]])))
    return np.stack(forward), np.stack(inverse)


def per_device(density, gain_left, gain_right, loss_kernel):
    forward, inverse = weights()
    held = (4, 2, 2, 2, 16, 128)
    far = pl.BlockSpec(memory_space=pltpu.HBM)
    vmem = pl.BlockSpec(memory_space=pltpu.VMEM)
    dma = pltpu.SemaphoreType.DMA
    landing = (pltpu.VMEM(held, f32), pltpu.VMEM(held, f32))
    return pl.pallas_call(
        kernel,
        out_shape=jax.ShapeDtypeStruct(density.shape, f32),
        in_specs=[far] * 6,
        out_specs=vmem,
        scratch_shapes=[
            pltpu.VMEM(density.shape, f32),
            pltpu.VMEM(gain_left.shape, f32),
            pltpu.VMEM(gain_right.shape, f32),
            pltpu.VMEM((1, loss_kernel.shape[0]), f32),
            pltpu.VMEM(forward.shape, bf16),
            pltpu.VMEM(inverse.shape, bf16),
            pltpu.VMEM(held, f32),
            landing,
            landing,
            pltpu.VMEM((CH, NP, 2, 2, 8, 128), f32),
            pltpu.VMEM((CH, M, 2, 8, 128), f32),
            pltpu.VMEM((CH, M, 2, 8, 128), f32),
            pltpu.VMEM(held, f32),
            pltpu.VMEM((9, M, 8, 256), f32),
            pltpu.VMEM((M, 2, 8, 256), f32),
            pltpu.VMEM((128, 256), f32),
            dma((2, CH, 4)),
            dma((2, CH, 4)),
            dma((CH, NP)),
            dma((CH, NP)),
            dma((CH, NP)),
            dma((CH, NP)),
            dma((2, CH)),
            dma((6,)),
            dma((CH, NP)),
            dma((CH, NP)),
            pltpu.SemaphoreType.REGULAR,
            pltpu.VMEM((2, 2, 2, 16, 128), f32),
            pltpu.VMEM((2, 2, 16, 128), f32),
            dma((2, 2)),
            dma((2,)),
            pltpu.SemaphoreType.REGULAR,
        ],
        compiler_params=pltpu.CompilerParams(
            collective_id=0, has_side_effects=True, vmem_limit_bytes=63 * 1024 * 1024
        ),
    )(density, gain_left, gain_right, loss_kernel.reshape(1, -1), jnp.asarray(forward), jnp.asarray(inverse))


def solution(mesh):
    in_specs = (P("space", None, None, "vel"), P(), P(), P())
    out_specs = P("space", None, None, "vel")
    return jax.shard_map(
        per_device, mesh=mesh, in_specs=in_specs, out_specs=out_specs, check_vma=False
    )
```
